256 devices in a mesh: dp: 64 (over z, x, core), mp: 4 (over y).
Axes of the slice: x: 4, y: 4, z: 8, core: 2. Of those that a mesh axis runs over, the one named last changes fastest.
Arguments:
- grad_parts: float32 [64, 2048, 2048], P('dp', None, 'mp'), may hold values from -16 to 16
- master: float32 [2048, 2048], P('dp', 'mp'), may hold values from -0.125 to 0.125
- moment_one: float32 [2048, 2048], P('dp', 'mp'), may hold values from -6 to 6
- moment_two: float32 [2048, 2048], P('dp', 'mp'), may hold values from 0.02 to 0.16
- states: bfloat16 [32768, 2048], P('dp'), may hold values from -6 to 6
- action_ids: int32 [32768, 4], P('dp'), may hold values from 0 to 255
- env_counts: int32 [64], P('dp'), may hold values from 256 to 512, as said below
- owners: int32 [32768, 1], P('dp'), may hold values from 0 to 63; in each aligned block of 512 rows (0 to 511, 512 to 1023, ...) at most 12 rows name the same one
- act_table: bfloat16 [256, 2048], replicated, may hold values from -6 to 6
- norm_gain: float32 [2048], replicated, may hold values from 0.1 to 1.9
- head: bfloat16 [2048, 256], P(None, 'mp'), may hold values from -0.125 to 0.125
Outputs:
- moment_one_new: float32 [2048, 2048], P('dp', 'mp')
- moment_two_new: float32 [2048, 2048], P('dp', 'mp')
- master_new: float32 [2048, 2048], P('dp', 'mp')
- logits: float32 [32768, 256], P('dp', 'mp')
- received: bfloat16 [49152, 2048], P('dp', 'mp')
The draws below stay inside these ranges and needn't reach their ends.
Inputs may be any that keep to these rules, and one draw needn't show every extreme that they name: `env_counts`: every actor has at least half of its slots live, and some actor has all 512 live. `owners`: among the rows of one actor at most 12 name the same owner, and some actor's rows reach 12 for some owner.
All inputs are finite; a program needn't handle non-finite values.
Results may differ from the reference program's by a relative error of at most 0.017.
Values may be sent and summed in bfloat16 or wider, within the bound.
No kernel may reach another device: no remote copies, remote signals or barrier semaphores. Data moves between devices by JAX's collectives and lax.ppermute only.
A program may use at most 64 MiB of HBM per device.

```python
import math
import jax
import jax.numpy as jnp
import numpy as np
from jax import lax

D = 2048
ACTIONS = 256
ENVS_DEV = 512
STEPS = 4
ENVS = 32768
CAP = 12
N_DP = 64


def draw_env_counts(key, part):
    actors = ENVS // ENVS_DEV
    key_base = jax.random.fold_in(key, 11)
    key_full = jax.random.fold_in(key, 12)
    key_pick = jax.random.fold_in(key, 13)
    base = jax.random.randint(key_base, (actors,), ENVS_DEV // 2, ENVS_DEV + 1)
    full_marks = jax.random.randint(key_full, (actors,), 0, 8) == 0
    chosen = jax.random.randint(key_pick, (), 0, actors)
    picked = jnp.arange(actors, dtype=jnp.int32) == chosen
    return jnp.where(full_marks | picked, ENVS_DEV, base).astype(jnp.int32)


def set_ends(result, stream_key, least, high):
    place = [jax.random.randint(jax.random.fold_in(stream_key, axis), (), 0, length) for axis, length in enumerate(result.shape)]
    longest = result.shape.index(max(result.shape))
    beside = place[:longest] + [(place[longest] + 1) % result.shape[longest]] + place[longest + 1:]
    return result.at[tuple(place)].set(least).at[tuple(beside)].set(high)


def with_spikes(entries, rng, source, target, parts, factor):
    def block_of(position):
        return (jnp.arange(entries.shape[position]) // (entries.shape[position] // parts)).reshape((-1,) + (1,) * (entries.ndim - 1 - position))

    near = jax.random.permutation(rng, parts)[block_of(target)]
    far = (block_of(target) + parts // 2) % parts
    return jnp.where((block_of(source) == near) | (block_of(source) == far), factor * entries, entries)


def block_scale(rng, dims, cuts, low, largest):
    def one(position, shards_of):
        steps = jax.random.uniform(jax.random.fold_in(jax.random.fold_in(rng, 6), position), (shards_of,), jnp.float32, low / len(cuts), largest / len(cuts))
        return jnp.repeat(jnp.exp(steps), dims[position] // shards_of).reshape((-1,) + (1,) * (len(dims) - position - 1))

    factor_of = one(*cuts[0])
    for cut in cuts[1:]:
        factor_of = factor_of * one(*cut)
    return factor_of


def deal_out(stream_key, own, number, rows, number_of, top, limit, slope):
    sequence = jax.random.permutation(stream_key, number_of)
    crowded, ordinary = shares(number_of, rows * top, limit, slope, True), shares(number_of, rows * top, limit, slope, False)
    places = jnp.arange(number_of)

    def named(tallies, rotation):
        used = int((tallies > 0).sum())
        fixed = max(1, used // 4)
        shifted = fixed + (places - fixed + rotation * (used - fixed)) % max(1, number_of - fixed)
        return jnp.zeros((number_of,), jnp.int32).at[sequence[jnp.where(places < fixed, places, shifted)]].set(jnp.asarray(tallies, jnp.int32))

    tallies = jnp.where(number % 4 == 0, named(crowded, number // 4), named(ordinary, number - number // 4 - 1))
    mixed = jax.random.permutation(jax.random.fold_in(own, 3), number_of)
    giver, sink = mixed[0:number_of // 2 * 2:2], mixed[1:number_of // 2 * 2:2]
    margin = jnp.minimum(tallies[giver] - 1, limit - tallies[sink]) // 2
    margin = jnp.where((giver == sequence[0]) | (sink == sequence[0]) | (tallies[sink] == 0), 0, jnp.maximum(margin, 0))
    shifted = jax.random.randint(jax.random.fold_in(own, 4), (number_of // 2,), 0, 1 << 20) % (margin + 1)
    tallies = tallies.at[giver].add(-shifted).at[sink].add(shifted)
    labels = jnp.searchsorted(jnp.cumsum(tallies), jnp.arange(rows * top), side="right").astype(jnp.int32)
    grid = labels.reshape(top, rows).T
    grid = grid[jax.random.permutation(jax.random.fold_in(own, 1), rows)]
    rotation = jax.random.randint(jax.random.fold_in(own, 2), (rows, 1), 0, top)
    return jnp.take_along_axis(grid, (jnp.arange(top)[None, :] + rotation) % top, axis=1)


def shares(count, total, most, skew, full):
    weights = [(1 << 20) // math.isqrt(standing ** skew) + 1 for standing in range(1, count + 1)]
    largest = most if full else min(most, max(-(-total // count), total * weights[0] // sum(weights)))
    least = 1 if total - largest >= count - 1 else 0
    counts, surplus = [largest] + [least] * (count - 1), total - largest - least * (count - 1)
    while surplus > 0:
        candidates = [i for i in range(1, count) if counts[i] < largest] or [i for i in range(1, count) if counts[i] < most]
        whole, left = sum([weights[i] for i in candidates]), surplus
        for i in candidates:
            addition = min(most - counts[i], max(1, left * weights[i] // whole), surplus)
            counts[i] = counts[i] + addition
            surplus = surplus - addition
    return np.array(counts)


def noise(own_key, extent, deviation, limit, cuts=(), held_as=jnp.bfloat16):
    entries = deviation * jax.random.normal(own_key, extent, jnp.float32)
    if cuts:
        entries = entries * block_scale(own_key, extent, cuts, -0.22, 0.18)
    return jnp.clip(entries, -limit, limit).astype(held_as)


def gaussian_with(stream_key, shape, scale, most, shards, heavy, held_as=jnp.bfloat16):
    values = scale * jax.random.normal(stream_key, shape, jnp.float32)
    if shards:
        values = values * block_scale(stream_key, shape, shards, -0.22, 0.18)
    return jnp.clip(with_spikes(values, jax.random.fold_in(stream_key, 3), *heavy), -most, most).astype(held_as)


def setup_inputs(seed: int = 0) -> dict:
    key_of = jax.random.split(jax.random.key(seed), 12)
    grad_parts = gaussian_with(key_of[0], (N_DP, D, D), 1.0, 16.0, ((0, 64), (2, 4)), (0, 1, 64, 4.0), jnp.float32)
    master = noise(key_of[1], (D, D), D ** -0.5, 0.125, ((0, 64), (1, 4)), jnp.float32)
    moment_one = noise(key_of[2], (D, D), 1.0, 6.0, ((0, 64), (1, 4)), jnp.float32)
    moment_two = jnp.clip(jnp.exp(math.log(0.16) - 2.0794415 * jax.random.uniform(key_of[3], (D, D), jnp.float32) ** block_scale(key_of[3], (D, D), ((0, 64), (1, 4)), -0.2, 0.2)), 0.02, 0.16)
    states = noise(key_of[4], (ENVS, D), 1.0, 6.0, ((0, 64),))
    action_ids = set_ends(jax.random.randint(key_of[5], (ENVS, STEPS), 0, ACTIONS), jax.random.fold_in(key_of[5], 1), 0, ACTIONS - 1).astype(jnp.int32)
    env_counts = draw_env_counts(jax.random.fold_in(key_of[11], 71), 0)
    owners_keys = jax.random.split(jax.random.fold_in(key_of[7], 1), ENVS // ENVS_DEV)
    owners_turns = jax.random.permutation(jax.random.fold_in(key_of[7], 3), ENVS // ENVS_DEV)
    owners = jax.vmap(lambda own, number: deal_out(jax.random.fold_in(key_of[7], 2), own, number, ENVS_DEV, N_DP, 1, CAP, 2))(owners_keys, owners_turns).reshape((ENVS, 1))
    act_table = noise(key_of[8], (ACTIONS, D), 1.0, 6.0)
    norm_gain = jnp.clip(1.0 + 0.18 * jax.random.normal(key_of[9], (D,), jnp.float32), 0.1, 1.9)
    head = noise(key_of[10], (D, ACTIONS), D ** -0.5, 0.125, ((1, 4),))
    return {"grad_parts": grad_parts, "master": master, "moment_one": moment_one, "moment_two": moment_two, "states": states, "action_ids": action_ids, "env_counts": env_counts, "owners": owners, "act_table": act_table, "norm_gain": norm_gain, "head": head}


beta_one = 0.9
beta_two = 0.999
corr_one = 1.0 - 0.9 ** 10
corr_two = 1.0 - 0.999 ** 10
rate_lr = 0.01
adam_eps = 1e-08
norm_eps = 1e-06

def reference(grad_parts, master, moment_one, moment_two, states, action_ids, env_counts, owners, act_table, norm_gain, head):
    gradient = lax.optimization_barrier(jnp.sum(grad_parts, axis=0))
    m_new = beta_one * moment_one + (1.0 - beta_one) * gradient
    v_new = beta_two * moment_two + (1.0 - beta_two) * gradient * gradient
    w_new = master - rate_lr * (m_new / corr_one) / (jnp.sqrt(v_new / corr_two) + adam_eps)
    weights = w_new.astype(jnp.bfloat16)
    envs = states.shape[0]
    per_dev = envs // N_DP
    width = states.shape[1]
    actions_num = act_table.shape[0]

    def decode(block):
        state, ids = block
        for step_idx in range(STEPS):
            onehot = (ids[:, step_idx][:, None] == jnp.arange(actions_num, dtype=jnp.int32)[None, :]).astype(jnp.bfloat16)
            embedded = jnp.dot(onehot, act_table, preferred_element_type=jnp.float32)
            hidden = (state.astype(jnp.float32) + embedded).astype(jnp.bfloat16)
            mixed = jnp.dot(hidden, weights, preferred_element_type=jnp.float32).astype(jnp.bfloat16)
            mixed_f = mixed.astype(jnp.float32)
            inverse = lax.rsqrt(lax.optimization_barrier(jnp.mean(mixed_f * mixed_f, axis=1)) + norm_eps)
            state = (state.astype(jnp.float32) + norm_gain[None, :] * mixed_f * inverse[:, None]).astype(jnp.bfloat16)
        scores = jnp.dot(state, head, preferred_element_type=jnp.float32)
        return (state, scores)
    final, scores = lax.map(decode, (states.reshape(N_DP, per_dev, width), action_ids.reshape(N_DP, per_dev, STEPS)))
    final = final.reshape(envs, width)
    scores = scores.reshape(envs, actions_num)
    local_idx = jnp.arange(per_dev, dtype=jnp.int32)
    active = (local_idx[None, :] < env_counts[:, None]).reshape(envs)
    logits = scores * active[:, None].astype(jnp.float32)
    target = owners[:, 0].astype(jnp.int32)
    capacity = max(2, 3 * per_dev // (2 * N_DP))
    marks = ((target[:, None] == jnp.arange(N_DP, dtype=jnp.int32)[None, :]) & active[:, None]).astype(jnp.int32)
    marks = marks.reshape(N_DP, per_dev, N_DP)
    ranked = jnp.cumsum(marks, axis=1) - marks
    slot_idx = lax.optimization_barrier(jnp.sum(ranked * marks, axis=2)).reshape(envs)
    source = jnp.arange(envs, dtype=jnp.int32) // per_dev
    total_rows = N_DP * N_DP * capacity
    index = jnp.where(active, target * (N_DP * capacity) + source * capacity + slot_idx, total_rows).astype(jnp.int32)
    received = jnp.zeros((total_rows, width), jnp.bfloat16).at[index].set(final, mode='drop')
    return (m_new, v_new, w_new, logits, received)
```

```python
import jax
import jax.numpy as jnp
from jax import lax
from jax.sharding import Mesh, PartitionSpec as P

STEPS = 4
NZ, NX, NC, NY = 8, 4, 2, 4
DP = ("z", "x", "c")

beta_one = 0.9
beta_two = 0.999
corr_one = 1.0 - 0.9**10
corr_two = 1.0 - 0.999**10
rate_lr = 0.01
adam_eps = 1e-08
norm_eps = 1e-06
F32 = jnp.float32
BF16 = jnp.bfloat16


def exchange(v, axis):
    return lax.all_to_all(v, axis, 0, 0, tiled=True)


def spread(v, axis, n):
    return exchange(jnp.broadcast_to(v[None], (n,) + v.shape), axis)


def swap(v):
    return lax.ppermute(v, "c", [(0, 1), (1, 0)])


def reduce_part(g):
    me = lax.axis_index("c")
    give = lax.dynamic_index_in_dim(g, 1 - me, 2, keepdims=False).astype(BF16)
    keep = lax.dynamic_index_in_dim(g, me, 2, keepdims=False)
    both = (keep + swap(give).astype(F32)).astype(BF16)
    both = jnp.transpose(both, (1, 0, 2, 3))
    by_x = exchange(both, "x").astype(F32).sum(0).astype(BF16)
    return exchange(by_x, "z").astype(F32).sum(0)


def body(
    grad_parts,
    master,
    moment_one,
    moment_two,
    states,
    action_ids,
    env_counts,
    owners,
    act_table,
    norm_gain,
    head,
):
    width, cols = grad_parts.shape[1:]
    rows = width // (NZ * NX * NC)
    half = cols // 2
    env_slots = states.shape[0]
    actions_num = act_table.shape[0]
    owner_num = NZ * NX * NC
    capacity = max(2, 3 * env_slots // (2 * owner_num))
    share = capacity // NY
    my_y = lax.axis_index("y")

    active = jnp.arange(env_slots, dtype=jnp.int32) < env_counts[0]
    target = owners[:, 0]
    marks = (
        (target[:, None] == jnp.arange(owner_num, dtype=jnp.int32)[None, :]) & active[:, None]
    ).astype(jnp.int32)
    ranked = jnp.cumsum(marks, axis=0) - marks
    slot_idx = jnp.sum(ranked * marks, axis=1)
    mine = active & (slot_idx // share == my_y)
    place = jnp.where(mine, target * share + slot_idx - my_y * share, -1)
    pick = (jnp.arange(owner_num * share, dtype=jnp.int32)[:, None] == place[None, :]).astype(BF16)
    tags = jnp.pad((action_ids + 1).astype(BF16), ((0, 0), (0, 128 - STEPS)))
    outgoing = jnp.dot(pick, jnp.concatenate([states, tags], 1), preferred_element_type=F32)
    outgoing = outgoing.astype(BF16).reshape(owner_num, share, width + 128)
    heads = lax.all_gather(head, "y", axis=0)

    g = grad_parts[0].reshape(NZ, NX, NC, rows, cols)
    parts = []
    for h in range(2):
        sl = slice(h * half, (h + 1) * half)
        gradient = reduce_part(g[..., sl])
        m_new = beta_one * moment_one[:, sl] + (1.0 - beta_one) * gradient
        v_new = beta_two * moment_two[:, sl] + (1.0 - beta_two) * gradient * gradient
        w_new = master[:, sl] - rate_lr * (m_new / corr_one) / (
            jnp.sqrt(v_new / corr_two) + adam_eps
        )
        parts.append((m_new, v_new, w_new, spread(w_new.astype(BF16), "z", NZ)))
    m_new, v_new, w_new = (jnp.concatenate([parts[0][i], parts[1][i]], 1) for i in range(3))
    wa, wb = parts[0][3], parts[1][3]
    wa, wb, outgoing = lax.optimization_barrier((wa, wb, outgoing))
    arrived = exchange(outgoing, DP)
    wa = spread(spread(wa, "x", NX), "y", NY)
    wb = spread(spread(wb, "y", NY), "x", NX)
    both = jnp.stack([wa, jnp.transpose(wb, (1, 0, 2, 3, 4))])
    other = swap(both)
    me = lax.axis_index("c")
    weights = jnp.where(me == 0, jnp.stack([both, other]), jnp.stack([other, both]))
    weights = jnp.transpose(weights, (4, 3, 0, 5, 2, 1, 6)).reshape(width, NY * cols)

    own = env_slots // NY
    arrived = arrived.reshape(owner_num * share, width + 128)
    slot_ids = arrived[:, width : width + STEPS].astype(jnp.int32) - 1
    env_ids = lax.dynamic_slice_in_dim(action_ids, my_y * own, own, 0)
    ids = jnp.concatenate([slot_ids, env_ids], 0)
    state = jnp.concatenate(
        [arrived[:, :width], lax.dynamic_slice_in_dim(states, my_y * own, own, 0)], 0
    )
    action_iota = jnp.arange(actions_num, dtype=jnp.int32)
    for step_idx in range(STEPS):
        onehot = (ids[:, step_idx][:, None] == action_iota[None, :]).astype(BF16)
        embedded = jnp.dot(onehot, act_table, preferred_element_type=F32)
        hidden = (state.astype(F32) + embedded).astype(BF16)
        mixed_f = jnp.dot(hidden, weights, preferred_element_type=F32).astype(BF16).astype(F32)
        inverse = lax.rsqrt(jnp.mean(mixed_f * mixed_f, axis=1) + norm_eps)
        state = (state.astype(F32) + norm_gain[None, :] * mixed_f * inverse[:, None]).astype(BF16)
    slots = owner_num * share
    kept = jnp.where(slot_ids[:, :1] >= 0, state[:slots], jnp.zeros((), BF16))
    landed = exchange(jnp.transpose(kept.reshape(slots, NY, cols), (1, 0, 2)), "y")
    row = jnp.arange(owner_num * capacity, dtype=jnp.int32)
    at = (row % capacity) // share * slots + row // capacity * share + row % share
    order = (at[:, None] == row[None, :]).astype(BF16)
    received = jnp.dot(order, landed.reshape(owner_num * capacity, cols), preferred_element_type=F32)

    scores = jnp.einsum("rd,jda->jra", state[slots:], heads, preferred_element_type=F32)
    scores = exchange(scores, "y").reshape(env_slots, head.shape[1])
    logits = scores * active[:, None].astype(F32)
    return (m_new, v_new, w_new, logits, received.astype(BF16))


def solution(mesh):
    grid = Mesh(mesh.devices.reshape(NZ, NX, NC, NY), DP + ("y",))
    in_specs = (
        P(DP, None, "y"),
        P(DP, "y"),
        P(DP, "y"),
        P(DP, "y"),
        P(DP, None),
        P(DP, None),
        P(DP),
        P(DP, None),
        P(),
        P(),
        P(None, "y"),
    )
    out_specs = (P(DP, "y"),) * 5
    return jax.shard_map(body, mesh=grid, in_specs=in_specs, out_specs=out_specs, check_vma=False)
```

```python
import functools

import jax
import jax.numpy as jnp
from jax import lax
from jax.experimental import pallas as pl
from jax.experimental.pallas import tpu as pltpu
from jax.sharding import Mesh, PartitionSpec as P

STEPS = 4
NZ, NX, NC, NY = 8, 4, 2, 4
DP = ("z", "x", "c")
TAGS = 128

beta_one = 0.9
beta_two = 0.999
corr_one = 1.0 - 0.9**10
corr_two = 1.0 - 0.999**10
rate_lr = 0.01
adam_eps = 1e-08
norm_eps = 1e-06
F32 = jnp.float32
BF16 = jnp.bfloat16


def exchange(v, axis):
    return lax.all_to_all(v, axis, 0, 0, tiled=True)


def shift(v, axis, k, n):
    if k == 0:
        return v
    return lax.ppermute(v, axis, [(i, (i + k) % n) for i in range(n)])


def swap(v):
    return shift(v, "c", 1, NC)


def give_kernel(where, g_ref, out_ref):
    out_ref[0] = g_ref[:, 0, 0].astype(BF16)


def keep_kernel(where, g_ref, got_ref, out_ref):
    out_ref[0] = (g_ref[:, 0, 0] + got_ref[0].astype(F32)).astype(BF16)


def rows_of_core(kernel, core, g, *rest):
    nz, nx, _, rows, cols = g.shape
    block = pl.BlockSpec((1, nz, rows, cols), lambda i, where: (i, 0, 0, 0))
    return pl.pallas_call(
        kernel,
        grid_spec=pltpu.PrefetchScalarGridSpec(
            num_scalar_prefetch=1,
            grid=(nx,),
            in_specs=[
                pl.BlockSpec((nz, 1, 1, rows, cols), lambda i, where: (0, i, where[0], 0, 0)),
                *[block for _ in rest],
            ],
            out_specs=block,
        ),
        out_shape=jax.ShapeDtypeStruct((nx, nz, rows, cols), BF16),
        compiler_params=pltpu.CompilerParams(vmem_limit_bytes=24 * 2**20),
    )(core, g, *rest)


def decode_kernel(with_logits, m, width, place, rows_ref, table_ref, gain_ref, *refs):
    n_pieces = 4 * NY
    if with_logits:
        head_ref, refs = refs[0], refs[1:]
    pieces, (out_ref, w_ref, hidden, mixed, state, sems) = refs[:n_pieces], refs[n_pieces:]
    my_x, my_c, my_y = place[0], place[1], place[2]
    blocks, wide = w_ref.shape[0], w_ref.shape[-1]
    copies = []
    for p in range(n_pieces):
        second, k, other = p // (2 * NY), p % (2 * NY) // 2, p % 2
        core = lax.rem(my_c + other, NC)
        for i in range(NX):
            x_off, y_off = (k, i) if second else (i, k)
            x = lax.rem(my_x - x_off + NX, NX)
            y = lax.rem(my_y - y_off + NY, NY)
            copy = pltpu.make_async_copy(
                pieces[p].at[i], w_ref.at[2 * y + second, :, x, core], sems.at[p * NX + i]
            )
            copy.start()
            copies.append(copy)

    actions = table_ref.shape[0]
    number = lax.broadcasted_iota(jnp.int32, (m, actions), 1) + 1

    def embed(step, n, old):
        tag = rows_ref[:, width + step : width + step + 1].astype(jnp.int32)
        onehot = jnp.where(tag == number, 1.0, 0.0).astype(BF16)
        at = pl.ds(n * wide, wide)
        embedded = jnp.dot(onehot, table_ref[:, at], preferred_element_type=F32)
        hidden[:, at] = (old.astype(F32) + embedded).astype(BF16)

    for n in range(blocks):
        embed(0, n, rows_ref[:, n * wide : (n + 1) * wide])
    for copy in copies:
        copy.wait()
    for step in range(STEPS):

        def multiply(i, total):
            for half in range(2):
                n = 2 * i + half
                w = w_ref[n].reshape(width, wide)
                got = jnp.dot(hidden[...], w, preferred_element_type=F32).astype(BF16)
                mixed[:, pl.ds(pl.multiple_of(n * wide, wide), wide)] = got
                got = got.astype(F32)
                total = total + jnp.sum(got * got, axis=1, keepdims=True)
            return total

        total = lax.fori_loop(0, blocks // 2, multiply, jnp.zeros((m, 1), F32))
        inverse = lax.rsqrt(total * (1.0 / width) + norm_eps)
        for n in range(blocks):
            at = slice(n * wide, (n + 1) * wide)
            old = rows_ref[:, at] if step == 0 else state[:, at]
            new = old.astype(F32) + gain_ref[:, at] * mixed[:, at].astype(F32) * inverse
            new = new.astype(BF16)
            if step < STEPS - 1:
                state[:, at] = new
                embed(step + 1, n, new)
            elif with_logits:
                state[:, at] = new
            else:
                k = lax.rem(n // 2 - my_y + NY, NY)
                out_ref[k, :, n % 2 * wide : (n % 2 + 1) * wide] = new
    if with_logits:
        scores = jnp.dot(state[...], head_ref[...], preferred_element_type=F32)
        row = my_y * m + lax.broadcasted_iota(jnp.int32, scores.shape, 0)
        out_ref[...] = scores * jnp.where(row < place[3], 1.0, 0.0)


def decode(place, rows, table, gain, pieces, head=None):
    m, width = rows.shape[0], table.shape[1]
    wide = width // NY // 2
    vmem = pl.BlockSpec(memory_space=pltpu.VMEM)
    if head is None:
        out = jax.ShapeDtypeStruct((NY, m, width // NY), BF16)
    else:
        out = jax.ShapeDtypeStruct((m, head.shape[1]), F32)
    extra = [] if head is None else [head]
    return pl.pallas_call(
        functools.partial(decode_kernel, head is not None, m, width),
        in_specs=[pl.BlockSpec(memory_space=pltpu.SMEM)]
        + [vmem] * (3 + len(extra))
        + [pl.BlockSpec(memory_space=pl.ANY)] * len(pieces),
        out_specs=vmem,
        out_shape=out,
        scratch_shapes=[
            pltpu.VMEM((2 * NY, NZ, NX, NC, width // (NZ * NX * NC), wide), BF16),
            pltpu.VMEM((m, width), BF16),
            pltpu.VMEM((m, width), BF16),
            pltpu.VMEM((m, width), BF16),
            pltpu.SemaphoreType.DMA((len(pieces) * NX,)),
        ],
        compiler_params=pltpu.CompilerParams(vmem_limit_bytes=32 * 2**20),
        cost_estimate=pl.CostEstimate(
            flops=2 * STEPS * m * width * width, bytes_accessed=2 * width * width, transcendentals=0
        ),
    )(place, rows, table, gain, *extra, *pieces)


def body(
    grad_parts,
    master,
    moment_one,
    moment_two,
    states,
    action_ids,
    env_counts,
    owners,
    act_table,
    norm_gain,
    head,
):
    width, cols = grad_parts.shape[1:]
    rows = width // (NZ * NX * NC)
    half = cols // 2
    env_slots = states.shape[0]
    owner_num = NZ * NX * NC
    capacity = max(2, 3 * env_slots // (2 * owner_num))
    share = capacity // NY
    slots = owner_num * share
    own = env_slots // NY
    my_x, my_c, my_y = lax.axis_index("x"), lax.axis_index("c"), lax.axis_index("y")
    place = jnp.stack([my_x, my_c, my_y, env_counts[0]]).astype(jnp.int32)

    g = grad_parts[0].reshape(NZ, NX, NC, rows, cols)
    got = swap(rows_of_core(give_kernel, (1 - my_c)[None].astype(jnp.int32), g))
    both = rows_of_core(keep_kernel, my_c[None].astype(jnp.int32), g, got)
    by_x = exchange(both, "x").astype(F32).sum(0).astype(BF16)
    gradient = exchange(by_x, "z").astype(F32).sum(0)

    heads = jnp.concatenate([shift(head, "y", (NY - k) % NY, NY) for k in range(NY)], 1)

    active = jnp.arange(env_slots, dtype=jnp.int32) < env_counts[0]
    target = owners[:, 0]
    marks = (
        (target[:, None] == jnp.arange(owner_num, dtype=jnp.int32)[None, :]) & active[:, None]
    ).astype(jnp.int32)
    ranked = jnp.cumsum(marks, axis=0) - marks
    slot_idx = jnp.sum(ranked * marks, axis=1)
    mine = active & (slot_idx // share == my_y)
    index = jnp.where(mine, target * share + slot_idx - my_y * share, -1)
    pick = (jnp.arange(slots, dtype=jnp.int32)[:, None] == index[None, :]).astype(BF16)
    tags = jnp.pad((action_ids + 1).astype(BF16), ((0, 0), (0, TAGS - STEPS)))
    tagged = jnp.concatenate([states, tags], 1)
    outgoing = jnp.dot(pick, tagged, preferred_element_type=F32)
    outgoing = outgoing.astype(BF16).reshape(owner_num, share, width + TAGS)
    actor_rows = lax.dynamic_slice_in_dim(tagged, my_y * own, own, 0)

    m_new = beta_one * moment_one + (1.0 - beta_one) * gradient
    v_new = beta_two * moment_two + (1.0 - beta_two) * gradient * gradient
    w_new = master - rate_lr * (m_new / corr_one) / (jnp.sqrt(v_new / corr_two) + adam_eps)

    w = exchange(jnp.broadcast_to(w_new.astype(BF16)[None], (NZ, rows, cols)), "z")
    w, outgoing, actor_rows, heads = lax.optimization_barrier((w, outgoing, actor_rows, heads))
    first, second = w[..., :half], w[..., half:]
    first = jnp.stack([shift(first, "x", k, NX) for k in range(NX)])
    second = jnp.stack([shift(second, "y", k, NY) for k in range(NY)])
    arrived = exchange(outgoing, DP)
    pieces = []
    for v, axis, n in ((first, "y", NY), (second, "x", NX)):
        for k in range(n):
            piece = shift(v, axis, k, n)
            pieces += [piece, swap(piece)]

    slot_rows = arrived.reshape(slots, width + TAGS)
    gain = norm_gain[None, :]
    final = decode(place, slot_rows, act_table, gain, pieces)
    final, actor_rows = lax.optimization_barrier((final, actor_rows))
    landed = [shift(final[k], "y", k, NY) for k in range(NY)]
    scores = decode(place, actor_rows, act_table, gain, pieces, heads)

    each = head.shape[1]
    scores = [shift(scores[:, k * each : (k + 1) * each], "y", k, NY) for k in range(NY)]
    logits = jnp.zeros((env_slots, each), F32)
    for k in range(NY):
        start = lax.rem(my_y - k + NY, NY) * own
        logits = lax.dynamic_update_slice_in_dim(logits, scores[k], start, 0)

    row = jnp.arange(owner_num * capacity, dtype=jnp.int32)
    part = lax.rem(my_y - row % capacity // share + NY, NY)
    at = part * slots + row // capacity * share + row % share
    order = (at[:, None] == row[None, :]).astype(BF16)
    received = jnp.dot(order, jnp.concatenate(landed, 0), preferred_element_type=F32)
    return (m_new, v_new, w_new, logits, received.astype(BF16))


def solution(mesh):
    grid = Mesh(mesh.devices.reshape(NZ, NX, NC, NY), DP + ("y",))
    in_specs = (
        P(DP, None, "y"),
        P(DP, "y"),
        P(DP, "y"),
        P(DP, "y"),
        P(DP, None),
        P(DP, None),
        P(DP),
        P(DP, None),
        P(),
        P(),
        P(None, "y"),
    )
    out_specs = (P(DP, "y"),) * 5
    return jax.shard_map(body, mesh=grid, in_specs=in_specs, out_specs=out_specs, check_vma=False)
```

```python
import functools

import jax
import jax.numpy as jnp
from jax import lax
from jax.experimental import pallas as pl
from jax.experimental.pallas import tpu as pltpu
from jax.sharding import Mesh, PartitionSpec as P

STEPS = 4
NZ, NX, NC, NY = 8, 4, 2, 4
DP = ("z", "x", "c")
TAGS = 128
VMEM_LIMIT = 60 * 2**20

beta_one = 0.9
beta_two = 0.999
corr_one = 1.0 - 0.9**10
corr_two = 1.0 - 0.999**10
rate_lr = 0.01
adam_eps = 1e-08
norm_eps = 1e-06
F32 = jnp.float32
BF16 = jnp.bfloat16


def exchange(v, axis):
    return lax.all_to_all(v, axis, 0, 0, tiled=True)


def shift(v, axis, k, n):
    if k == 0:
        return v
    return lax.ppermute(v, axis, [(i, (i + k) % n) for i in range(n)])


def swap(v):
    return shift(v, "c", 1, NC)


def core_rows_kernel(add, core, g_ref, *refs):
    if add:
        got_ref, refs = refs[0], refs[1:]
    out_ref, part, got, done, in_sems, got_sems, out_sems = refs
    nx = part.shape[0]
    loads, extra, stores = [], [], []
    for i in range(nx):
        loads.append(pltpu.make_async_copy(g_ref.at[:, i, core[0]], part.at[i], in_sems.at[i]))
        loads[-1].start()
        if add:
            extra.append(pltpu.make_async_copy(got_ref.at[i], got.at[i], got_sems.at[i]))
            extra[-1].start()
    for i in range(nx):
        loads[i].wait()
        if add:
            extra[i].wait()
            done[i] = (part[i] + got[i].astype(F32)).astype(BF16)
        else:
            done[i] = part[i].astype(BF16)
        stores.append(pltpu.make_async_copy(done.at[i], out_ref.at[i], out_sems.at[i]))
        stores[-1].start()
    for store in stores:
        store.wait()


def core_rows(core, g, *got):
    nz, nx, _, rows, cols = g.shape
    hbm = pl.BlockSpec(memory_space=pl.ANY)
    return pl.pallas_call(
        functools.partial(core_rows_kernel, bool(got)),
        in_specs=[pl.BlockSpec(memory_space=pltpu.SMEM), hbm] + [hbm for _ in got],
        out_specs=hbm,
        out_shape=jax.ShapeDtypeStruct((nx, nz, rows, cols), BF16),
        scratch_shapes=[
            pltpu.VMEM((nx, nz, rows, cols), F32),
            pltpu.VMEM((nx, nz, rows, cols), BF16),
            pltpu.VMEM((nx, nz, rows, cols), BF16),
            pltpu.SemaphoreType.DMA((nx,)),
            pltpu.SemaphoreType.DMA((nx,)),
            pltpu.SemaphoreType.DMA((nx,)),
        ],
        compiler_params=pltpu.CompilerParams(vmem_limit_bytes=VMEM_LIMIT),
    )(core[None].astype(jnp.int32), g, *got)


def decode_kernel(width, place, slots_ref, envs_ref, table_ref, gain_ref, *refs):
    n_pieces = 4 * NY
    heads, refs = refs[:NY], refs[NY:]
    pieces, (out_ref, w_ref, hidden, mixed, state, sems) = refs[:n_pieces], refs[n_pieces:]
    my_x, my_c, my_y = place[0], place[1], place[2]
    blocks, wide = w_ref.shape[0], w_ref.shape[-1]
    slots, own = slots_ref.shape[0], envs_ref.shape[0]
    m = slots + own
    tail = out_ref.shape[1] - slots
    groups = ((slots_ref, slice(0, slots), slots), (envs_ref, slice(slots, m), own))
    copies = ([], [])
    for p in range(n_pieces):
        second, k, other = p // (2 * NY), p % (2 * NY) // 2, p % 2
        core = lax.rem(my_c + other, NC)
        for i in range(NX):
            x_off, y_off = (k, i) if second else (i, k)
            x = lax.rem(my_x - x_off + NX, NX)
            y = lax.rem(my_y - y_off + NY, NY)
            copy = pltpu.make_async_copy(
                pieces[p].at[i], w_ref.at[2 * y + second, :, x, core], sems.at[p * NX + i]
            )
            copy.start()
            copies[second].append(copy)

    actions = table_ref.shape[0]

    def onehot(step, ref, count):
        tag = ref[:, width + step : width + step + 1].astype(jnp.int32)
        number = lax.broadcasted_iota(jnp.int32, (count, actions), 1) + 1
        return jnp.where(tag == number, 1.0, 0.0).astype(BF16)

    def embed(step, n, old, ref, at, count):
        cols = slice(n * wide, (n + 1) * wide)
        embedded = jnp.dot(onehot(step, ref, count), table_ref[:, cols], preferred_element_type=F32)
        hidden[at, cols] = (old.astype(F32) + embedded).astype(BF16)

    for n in range(blocks):
        for ref, at, count in groups:
            embed(0, n, ref[:, n * wide : (n + 1) * wide], ref, at, count)
    for step in range(STEPS):
        total = jnp.zeros((m, 1), F32)
        for second in range(2):
            if step == 0:
                for copy in copies[second]:
                    copy.wait()

            def multiply(i, total):
                for pair in range(2):
                    n = 4 * i + 2 * pair + second
                    w = w_ref[n].reshape(width, wide)
                    got = jnp.dot(hidden[...], w, preferred_element_type=F32).astype(BF16)
                    mixed[:, pl.ds(pl.multiple_of(n * wide, wide), wide)] = got
                    got = got.astype(F32)
                    total = total + jnp.sum(got * got, axis=1, keepdims=True)
                return total

            total = lax.fori_loop(0, blocks // 4, multiply, total)
        inverse = lax.rsqrt(total * (1.0 / width) + norm_eps)
        for n in range(blocks):
            cols = slice(n * wide, (n + 1) * wide)
            for ref, at, count in groups:
                old = ref[:, cols] if step == 0 else state[at, cols]
                new = old.astype(F32) + gain_ref[:, cols] * mixed[at, cols].astype(F32) * inverse[at]
                new = new.astype(BF16)
                if step < STEPS - 1:
                    state[at, cols] = new
                    embed(step + 1, n, new, ref, at, count)
                elif ref is envs_ref:
                    state[at, cols] = new
                else:
                    out_ref[n // 2, :slots, n % 2 * wide : (n % 2 + 1) * wide] = new
    for k in range(NY):
        scores = lax.dot_general(
            state[slots:m, :],
            heads[k][...],
            (((1,), (1,)), ((), ())),
            preferred_element_type=F32,
        )
        row = my_y * own + lax.broadcasted_iota(jnp.int32, scores.shape, 0)
        scores = (scores * jnp.where(row < place[3], 1.0, 0.0)).astype(BF16)
        packed = [scores[i * tail : (i + 1) * tail] for i in range(own // tail)]
        out_ref[lax.rem(my_y + k, NY), slots:, :] = jnp.concatenate(packed, 1)


def decode(place, slot_rows, env_rows, table, gain, heads, pieces):
    slots, own, width = slot_rows.shape[0], env_rows.shape[0], table.shape[1]
    wide, m = width // NY // 2, slots + own
    tail = own * heads[0].shape[0] // (width // NY)
    vmem = pl.BlockSpec(memory_space=pltpu.VMEM)
    return pl.pallas_call(
        functools.partial(decode_kernel, width),
        in_specs=[pl.BlockSpec(memory_space=pltpu.SMEM)]
        + [vmem] * (4 + NY)
        + [pl.BlockSpec(memory_space=pl.ANY)] * len(pieces),
        out_specs=vmem,
        out_shape=jax.ShapeDtypeStruct((NY, slots + tail, width // NY), BF16),
        scratch_shapes=[
            pltpu.VMEM((2 * NY, NZ, NX, NC, width // (NZ * NX * NC), wide), BF16),
            pltpu.VMEM((m, width), BF16),
            pltpu.VMEM((m, width), BF16),
            pltpu.VMEM((m, width), BF16),
            pltpu.SemaphoreType.DMA((len(pieces) * NX,)),
        ],
        compiler_params=pltpu.CompilerParams(vmem_limit_bytes=VMEM_LIMIT),
        cost_estimate=pl.CostEstimate(
            flops=2 * STEPS * m * width * width, bytes_accessed=2 * width * width, transcendentals=0
        ),
    )(place, slot_rows, env_rows, table, gain, *heads, *pieces)


def body(
    grad_parts,
    master,
    moment_one,
    moment_two,
    states,
    action_ids,
    env_counts,
    owners,
    act_table,
    norm_gain,
    head,
):
    width, cols = grad_parts.shape[1:]
    rows = width // (NZ * NX * NC)
    half = cols // 2
    env_slots = states.shape[0]
    owner_num = NZ * NX * NC
    capacity = max(2, 3 * env_slots // (2 * owner_num))
    share = capacity // NY
    slots = owner_num * share
    own = env_slots // NY
    my_x, my_c, my_y = lax.axis_index("x"), lax.axis_index("c"), lax.axis_index("y")
    place = jnp.stack([my_x, my_c, my_y, env_counts[0]]).astype(jnp.int32)

    g = grad_parts[0].reshape(NZ, NX, NC, rows, cols)
    both = core_rows(my_c, g, swap(core_rows(1 - my_c, g)))
    both, head = lax.optimization_barrier((both, head))
    by_x = exchange(both, "x")
    heads = [shift(head.T, "y", (NY - k) % NY, NY) for k in range(NY)]
    by_x, heads, states = lax.optimization_barrier((by_x, heads, states))
    by_x = by_x.astype(F32).sum(0).astype(BF16)
    gradient = exchange(by_x, "z").astype(F32).sum(0)

    active = jnp.arange(env_slots, dtype=jnp.int32) < env_counts[0]
    target = owners[:, 0]
    marks = (
        (target[:, None] == jnp.arange(owner_num, dtype=jnp.int32)[None, :]) & active[:, None]
    ).astype(jnp.int32)
    ranked = jnp.cumsum(marks, axis=0) - marks
    slot_idx = jnp.sum(ranked * marks, axis=1)
    mine = active & (slot_idx // share == my_y)
    column = target // NC % NX
    ahead = lax.rem(column - my_x + NX, NX)
    group = target // (NC * NX) * NC + target % NC
    groups = NZ * NC
    index = jnp.where(mine, (ahead * groups + group - my_y) * share + slot_idx, -1)
    pick = (jnp.arange(slots, dtype=jnp.int32)[:, None] == index[None, :]).astype(BF16)
    tags = jnp.pad((action_ids + 1).astype(BF16), ((0, 0), (0, TAGS - STEPS)))
    tagged = jnp.concatenate([states, tags], 1)
    outgoing = jnp.dot(pick, tagged, preferred_element_type=F32).astype(BF16)
    span = groups * share
    outgoing = [shift(outgoing[k * span : (k + 1) * span], "x", k, NX) for k in range(NX)]
    deep = -(-NX * share // 16) * 16
    row = jnp.arange(groups * deep, dtype=jnp.int32)
    place_in, part = row % deep, row // deep
    from_row = place_in // share * span + part * share + place_in % share
    from_row = jnp.where(place_in < NX * share, from_row, -1)
    pick = (from_row[:, None] == jnp.arange(slots, dtype=jnp.int32)[None, :]).astype(BF16)
    outgoing = jnp.dot(pick, jnp.concatenate(outgoing, 0), preferred_element_type=F32)
    outgoing = outgoing.astype(BF16).reshape(groups, deep, width + TAGS)
    actor_rows = lax.dynamic_slice_in_dim(tagged, my_y * own, own, 0)

    m_new = beta_one * moment_one + (1.0 - beta_one) * gradient
    v_new = beta_two * moment_two + (1.0 - beta_two) * gradient * gradient
    w_new = master - rate_lr * (m_new / corr_one) / (jnp.sqrt(v_new / corr_two) + adam_eps)

    w = exchange(jnp.broadcast_to(w_new.astype(BF16)[None], (NZ, rows, cols)), "z")
    w, outgoing, actor_rows = lax.optimization_barrier((w, outgoing, actor_rows))
    first, second = w[..., :half], w[..., half:]
    first = jnp.stack([shift(first, "x", k, NX) for k in range(NX)])
    second = jnp.stack([shift(second, "y", k, NY) for k in range(NY)])
    arrived = exchange(outgoing, ("z", "c")).reshape(groups * deep, width + TAGS)
    row = jnp.arange(slots, dtype=jnp.int32)
    source, behind = row // share, lax.rem(my_x - row // share // NC % NX + NX, NX)
    from_row = (source // (NC * NX) * NC + source % NC) * deep + behind * share + row % share
    pick = (from_row[:, None] == jnp.arange(groups * deep, dtype=jnp.int32)[None, :]).astype(BF16)
    slot_rows = jnp.dot(pick, arrived, preferred_element_type=F32).astype(BF16)
    first, second = lax.optimization_barrier((first, second))
    moved = [shift(first, "y", k, NY) for k in range(1, NY)]
    moved += [shift(second, "x", k, NX) for k in range(1, NX)]
    moved, slot_rows = lax.optimization_barrier((moved, slot_rows))
    pieces = []
    for piece in [first, *moved[: NY - 1], second, *moved[NY - 1 :]]:
        pieces += [piece, swap(piece)]

    final = decode(place, slot_rows, actor_rows, act_table, norm_gain[None, :], heads, pieces)
    landed = exchange(final, "y")

    each = head.shape[1]
    scores = landed[:, slots:].astype(F32).reshape(NY, -1, cols // each, each)
    logits = jnp.transpose(scores, (0, 2, 1, 3)).reshape(env_slots, each)

    row = jnp.arange(owner_num * capacity, dtype=jnp.int32)
    at = row % capacity // share * slots + row // capacity * share + row % share
    order = (at[:, None] == row[None, :]).astype(BF16)
    landed = landed[:, :slots].reshape(owner_num * capacity, cols)
    received = jnp.dot(order, landed, preferred_element_type=F32)
    return (m_new, v_new, w_new, logits, received.astype(BF16))


def solution(mesh):
    grid = Mesh(mesh.devices.reshape(NZ, NX, NC, NY), DP + ("y",))
    in_specs = (
        P(DP, None, "y"),
        P(DP, "y"),
        P(DP, "y"),
        P(DP, "y"),
        P(DP, None),
        P(DP, None),
        P(DP),
        P(DP, None),
        P(),
        P(),
        P(None, "y"),
    )
    out_specs = (P(DP, "y"),) * 5
    return jax.shard_map(body, mesh=grid, in_specs=in_specs, out_specs=out_specs, check_vma=False)
```

```python
import functools

import jax
import jax.numpy as jnp
from jax import lax
from jax.experimental import pallas as pl
from jax.experimental.pallas import tpu as pltpu
from jax.sharding import Mesh, PartitionSpec as P

STEPS = 4
NZ, NX, NC, NY = 8, 4, 2, 4
DP = ("z", "x", "c")
TAGS = 128
VMEM_LIMIT = 60 * 2**20
PARTS = ((0, 0, 4), (1, 0, 4), (3, 0, 4), (2, 0, 2), (2, 2, 2))

beta_one = 0.9
beta_two = 0.999
corr_one = 1.0 - 0.9**10
corr_two = 1.0 - 0.999**10
rate_lr = 0.01
adam_eps = 1e-08
norm_eps = 1e-06
F32 = jnp.float32
BF16 = jnp.bfloat16


def exchange(v, axis):
    return lax.all_to_all(v, axis, 0, 0, tiled=True)


def shift(v, axis, k, n):
    if k == 0:
        return v
    return lax.ppermute(v, axis, [(i, (i + k) % n) for i in range(n)])


def swap(v):
    return shift(v, "c", 1, NC)


def core_rows_kernel(add, core, g_ref, *refs):
    if add:
        got_ref, refs = refs[0], refs[1:]
    out_ref, part, got, done, in_sems, got_sems, out_sems = refs
    nx = part.shape[0]
    loads, extra, stores = [], [], []
    for i in range(nx):
        loads.append(pltpu.make_async_copy(g_ref.at[:, i, core[0]], part.at[i], in_sems.at[i]))
        loads[-1].start()
        if add:
            extra.append(pltpu.make_async_copy(got_ref.at[i], got.at[i], got_sems.at[i]))
            extra[-1].start()
    for i in range(nx):
        loads[i].wait()
        if add:
            extra[i].wait()
            done[i] = (part[i] + got[i].astype(F32)).astype(BF16)
        else:
            done[i] = part[i].astype(BF16)
        stores.append(pltpu.make_async_copy(done.at[i], out_ref.at[i], out_sems.at[i]))
        stores[-1].start()
    for store in stores:
        store.wait()


def core_rows(core, g, *got):
    nz, nx, _, rows, cols = g.shape
    hbm = pl.BlockSpec(memory_space=pl.ANY)
    return pl.pallas_call(
        functools.partial(core_rows_kernel, bool(got)),
        in_specs=[pl.BlockSpec(memory_space=pltpu.SMEM), hbm] + [hbm for _ in got],
        out_specs=hbm,
        out_shape=jax.ShapeDtypeStruct((nx, nz, rows, cols), BF16),
        scratch_shapes=[
            pltpu.VMEM((nx, nz, rows, cols), F32),
            pltpu.VMEM((nx, nz, rows, cols), BF16),
            pltpu.VMEM((nx, nz, rows, cols), BF16),
            pltpu.SemaphoreType.DMA((nx,)),
            pltpu.SemaphoreType.DMA((nx,)),
            pltpu.SemaphoreType.DMA((nx,)),
        ],
        compiler_params=pltpu.CompilerParams(vmem_limit_bytes=VMEM_LIMIT),
    )(core[None].astype(jnp.int32), g, *got)


def decode_kernel(width, place, slots_ref, envs_ref, table_ref, gain_ref, *refs):
    n_pieces = 2 * len(PARTS) * NC
    heads, refs = refs[:NY], refs[NY:]
    pieces, (out_ref, w_ref, hidden, mixed, state, sems) = refs[:n_pieces], refs[n_pieces:]
    my_x, my_c, my_y = place[0], place[1], place[2]
    blocks, wide = w_ref.shape[0], w_ref.shape[-1]
    slots, own = slots_ref.shape[0], envs_ref.shape[0]
    m = slots + own
    tail = out_ref.shape[1] - slots
    copies = ([], [])
    for p in range(n_pieces):
        second, rest = divmod(p, len(PARTS) * NC)
        (k, begin, count), other = PARTS[rest // NC], rest % NC
        core = lax.rem(my_c + other, NC)
        for i in range(begin, begin + count):
            x_off, y_off = (k, i) if second else (i, k)
            x = lax.rem(my_x - x_off + NX, NX)
            y = lax.rem(my_y - y_off + NY, NY)
            copy = pltpu.make_async_copy(
                pieces[p].at[i - begin],
                w_ref.at[2 * y + second, :, x, core],
                sems.at[((second * NX + k) * NX + i) * NC + other],
            )
            copy.start()
            copies[second].append(copy)

    actions = table_ref.shape[0]
    number = lax.broadcasted_iota(jnp.int32, (m, actions), 1) + 1
    lanes = 128

    def onehot(step):
        tags = [ref[:, width + step : width + step + 1] for ref in (slots_ref, envs_ref)]
        tag = jnp.concatenate([t.astype(F32) for t in tags], 0).astype(jnp.int32)
        return jnp.where(tag == number, 1.0, 0.0).astype(BF16)

    def embed(hot, cols, old):
        embedded = jnp.dot(hot, table_ref[:, cols], preferred_element_type=F32)
        hidden[:, cols] = (old.astype(F32) + embedded).astype(BF16)

    hot = onehot(0)
    for n in range(blocks):
        cols = slice(n * wide, (n + 1) * wide)
        state[:slots, cols] = slots_ref[:, cols]
        state[slots:, cols] = envs_ref[:, cols]
        embed(hot, cols, state[:, cols])
    for step in range(STEPS):
        total = jnp.zeros((m, lanes), F32)
        for second in range(2):
            if step == 0:
                for copy in copies[second]:
                    copy.wait()

            def multiply(i, total):
                for pair in range(2):
                    n = 4 * i + 2 * pair + second
                    w = w_ref[n].reshape(width, wide)
                    got = jnp.dot(hidden[...], w, preferred_element_type=F32).astype(BF16)
                    mixed[:, n * wide : (n + 1) * wide] = got
                    got = got.astype(F32)
                    for at in range(0, wide, lanes):
                        total = total + got[:, at : at + lanes] * got[:, at : at + lanes]
                return total

            for i in range(blocks // 4):
                total = multiply(i, total)
        total = jnp.sum(total, axis=1, keepdims=True)
        inverse = lax.rsqrt(total * (1.0 / width) + norm_eps)
        if step < STEPS - 1:
            hot = onehot(step + 1)
        for n in range(blocks):
            cols = slice(n * wide, (n + 1) * wide)
            old = state[:, cols].astype(F32)
            new = old + gain_ref[:, cols] * mixed[:, cols].astype(F32) * inverse
            new = new.astype(BF16)
            if step < STEPS - 1:
                state[:, cols] = new
                embed(hot, cols, new)
            else:
                state[slots:, cols] = new[slots:]
                out_ref[n // 2, :slots, n % 2 * wide : (n % 2 + 1) * wide] = new[:slots]
    for k in range(NY):
        scores = lax.dot_general(
            state[slots:m, :],
            heads[k][...],
            (((1,), (1,)), ((), ())),
            preferred_element_type=F32,
        )
        row = my_y * own + lax.broadcasted_iota(jnp.int32, scores.shape, 0)
        scores = (scores * jnp.where(row < place[3], 1.0, 0.0)).astype(BF16)
        packed = [scores[i * tail : (i + 1) * tail] for i in range(own // tail)]
        out_ref[lax.rem(my_y + k, NY), slots:, :] = jnp.concatenate(packed, 1)


def decode(place, slot_rows, env_rows, table, gain, heads, pieces):
    slots, own, width = slot_rows.shape[0], env_rows.shape[0], table.shape[1]
    wide, m = width // NY // 2, slots + own
    tail = own * heads[0].shape[0] // (width // NY)
    vmem = pl.BlockSpec(memory_space=pltpu.VMEM)
    return pl.pallas_call(
        functools.partial(decode_kernel, width),
        in_specs=[pl.BlockSpec(memory_space=pltpu.SMEM)]
        + [vmem] * (4 + NY)
        + [pl.BlockSpec(memory_space=pl.ANY)] * len(pieces),
        out_specs=vmem,
        out_shape=jax.ShapeDtypeStruct((NY, slots + tail, width // NY), BF16),
        scratch_shapes=[
            pltpu.VMEM((2 * NY, NZ, NX, NC, width // (NZ * NX * NC), wide), BF16),
            pltpu.VMEM((m, width), BF16),
            pltpu.VMEM((m, width), BF16),
            pltpu.VMEM((m, width), BF16),
            pltpu.SemaphoreType.DMA((2 * NX * NX * NC,)),
        ],
        compiler_params=pltpu.CompilerParams(vmem_limit_bytes=VMEM_LIMIT),
        cost_estimate=pl.CostEstimate(
            flops=2 * STEPS * m * width * width, bytes_accessed=2 * width * width, transcendentals=0
        ),
    )(place, slot_rows, env_rows, table, gain, *heads, *pieces)


def body(
    grad_parts,
    master,
    moment_one,
    moment_two,
    states,
    action_ids,
    env_counts,
    owners,
    act_table,
    norm_gain,
    head,
):
    width, cols = grad_parts.shape[1:]
    rows = width // (NZ * NX * NC)
    half = cols // 2
    env_slots = states.shape[0]
    owner_num = NZ * NX * NC
    capacity = max(2, 3 * env_slots // (2 * owner_num))
    share = capacity // NY
    slots = owner_num * share
    own = env_slots // NY
    my_x, my_c, my_y = lax.axis_index("x"), lax.axis_index("c"), lax.axis_index("y")
    place = jnp.stack([my_x, my_c, my_y, env_counts[0]]).astype(jnp.int32)

    g = grad_parts[0].reshape(NZ, NX, NC, rows, cols)
    both = core_rows(my_c, g, swap(core_rows(1 - my_c, g)))
    both, head = lax.optimization_barrier((both, head))
    by_x = exchange(both, "x")
    head = head.T
    heads = [head, shift(head, "y", 3, NY), None, shift(head, "y", 1, NY)]
    by_x, heads[1], heads[3], states, head = lax.optimization_barrier(
        (by_x, heads[1], heads[3], states, head)
    )
    heads[2] = shift(head, "y", 2, NY)
    by_x = by_x.astype(F32).sum(0).astype(BF16)
    gradient = exchange(by_x, "z").astype(F32).sum(0)

    active = jnp.arange(env_slots, dtype=jnp.int32) < env_counts[0]
    target = owners[:, 0]
    marks = (
        (target[:, None] == jnp.arange(owner_num, dtype=jnp.int32)[None, :]) & active[:, None]
    ).astype(jnp.int32)
    ranked = jnp.cumsum(marks, axis=0) - marks
    slot_idx = jnp.sum(ranked * marks, axis=1)
    mine = active & (slot_idx // share == my_y)
    column = target // NC % NX
    ahead = lax.rem(column - my_x + NX, NX)
    group = target // (NC * NX) * NC + target % NC
    groups = NZ * NC
    index = jnp.where(mine, (ahead * groups + group - my_y) * share + slot_idx, -1)
    pick = (jnp.arange(slots, dtype=jnp.int32)[:, None] == index[None, :]).astype(BF16)
    tags = jnp.pad((action_ids + 1).astype(BF16), ((0, 0), (0, TAGS - STEPS)))
    tagged = jnp.concatenate([states, tags], 1)
    outgoing = jnp.dot(pick, tagged, preferred_element_type=F32).astype(BF16)
    span = groups * share
    outgoing = [shift(outgoing[k * span : (k + 1) * span], "x", k, NX) for k in range(NX)]
    deep = -(-NX * share // 16) * 16
    row = jnp.arange(groups * deep, dtype=jnp.int32)
    place_in, part = row % deep, row // deep
    from_row = place_in // share * span + part * share + place_in % share
    from_row = jnp.where(place_in < NX * share, from_row, -1)
    pick = (from_row[:, None] == jnp.arange(slots, dtype=jnp.int32)[None, :]).astype(BF16)
    outgoing = jnp.dot(pick, jnp.concatenate(outgoing, 0), preferred_element_type=F32)
    outgoing = outgoing.astype(BF16).reshape(groups, deep, width + TAGS)
    actor_rows = lax.dynamic_slice_in_dim(tagged, my_y * own, own, 0)

    m_new = beta_one * moment_one + (1.0 - beta_one) * gradient
    v_new = beta_two * moment_two + (1.0 - beta_two) * gradient * gradient
    w_new = master - rate_lr * (m_new / corr_one) / (jnp.sqrt(v_new / corr_two) + adam_eps)

    w = exchange(jnp.broadcast_to(w_new.astype(BF16)[None], (NZ, rows, cols)), "z")
    w, outgoing, actor_rows, heads = lax.optimization_barrier((w, outgoing, actor_rows, heads))
    first, second = w[..., :half], w[..., half:]
    first = jnp.stack([shift(first, "x", k, NX) for k in range(NX)])
    second = jnp.stack([shift(second, "y", k, NY) for k in range(NY)])
    arrived = exchange(outgoing, ("z", "c")).reshape(groups * deep, width + TAGS)
    row = jnp.arange(slots, dtype=jnp.int32)
    source, behind = row // share, lax.rem(my_x - row // share // NC % NX + NX, NX)
    from_row = (source // (NC * NX) * NC + source % NC) * deep + behind * share + row % share
    pick = (from_row[:, None] == jnp.arange(groups * deep, dtype=jnp.int32)[None, :]).astype(BF16)
    slot_rows = jnp.dot(pick, arrived, preferred_element_type=F32).astype(BF16)
    first, second = lax.optimization_barrier((first, second))
    near = [shift(v, axis, k, NX) for v, axis in ((first, "y"), (second, "x")) for k in (1, 3)]
    near = lax.optimization_barrier(near)
    far = []
    for (back, front), axis in ((near[:2], "y"), (near[2:], "x")):
        far += [shift(back[: NX // 2], axis, 1, NX), shift(front[NX // 2 :], axis, 3, NX)]
    far, slot_rows = lax.optimization_barrier((far, slot_rows))
    pieces = []
    for piece in [first, *near[:2], *far[:2], second, *near[2:], *far[2:]]:
        pieces += [piece, swap(piece)]

    final = decode(place, slot_rows, actor_rows, act_table, norm_gain[None, :], heads, pieces)
    landed = exchange(final, "y")

    each = head.shape[0]
    scores = landed[:, slots:].astype(F32).reshape(NY, -1, cols // each, each)
    logits = jnp.transpose(scores, (0, 2, 1, 3)).reshape(env_slots, each)

    row = jnp.arange(owner_num * capacity, dtype=jnp.int32)
    at = row % capacity // share * slots + row // capacity * share + row % share
    order = (at[:, None] == row[None, :]).astype(BF16)
    landed = landed[:, :slots].reshape(owner_num * capacity, cols)
    received = jnp.dot(order, landed, preferred_element_type=F32)
    return (m_new, v_new, w_new, logits, received.astype(BF16))


def solution(mesh):
    grid = Mesh(mesh.devices.reshape(NZ, NX, NC, NY), DP + ("y",))
    in_specs = (
        P(DP, None, "y"),
        P(DP, "y"),
        P(DP, "y"),
        P(DP, "y"),
        P(DP, None),
        P(DP, None),
        P(DP),
        P(DP, None),
        P(),
        P(),
        P(None, "y"),
    )
    out_specs = (P(DP, "y"),) * 5
    return jax.shard_map(body, mesh=grid, in_specs=in_specs, out_specs=out_specs, check_vma=False)
```

```python
import functools

import jax
import jax.numpy as jnp
from jax import lax
from jax.experimental import pallas as pl
from jax.experimental.pallas import tpu as pltpu
from jax.sharding import Mesh, PartitionSpec as P

STEPS = 4
NZ, NX, NC, NY = 8, 4, 2, 4
DP = ("z", "x", "c")
TAGS = 128
VMEM_LIMIT = 60 * 2**20
PARTS = ((0, 0, 4), (1, 0, 4), (3, 0, 4), (2, 0, 2), (2, 2, 2))

beta_one = 0.9
beta_two = 0.999
corr_one = 1.0 - 0.9**10
corr_two = 1.0 - 0.999**10
rate_lr = 0.01
adam_eps = 1e-08
norm_eps = 1e-06
F32 = jnp.float32
BF16 = jnp.bfloat16


def exchange(v, axis):
    return lax.all_to_all(v, axis, 0, 0, tiled=True)


def shift(v, axis, k, n):
    if k == 0:
        return v
    return lax.ppermute(v, axis, [(i, (i + k) % n) for i in range(n)])


def swap(v):
    return shift(v, "c", 1, NC)


def core_rows_kernel(add, core, g_ref, *refs):
    if add:
        got_ref, refs = refs[0], refs[1:]
    out_ref, part, got, done, in_sems, got_sems, out_sems = refs
    nx = part.shape[0]
    loads, extra, stores = [], [], []
    for i in range(nx):
        loads.append(pltpu.make_async_copy(g_ref.at[:, i, core[0]], part.at[i], in_sems.at[i]))
        loads[-1].start()
        if add:
            extra.append(pltpu.make_async_copy(got_ref.at[i], got.at[i], got_sems.at[i]))
            extra[-1].start()
    for i in range(nx):
        loads[i].wait()
        if add:
            extra[i].wait()
            done[i] = (part[i] + got[i].astype(F32)).astype(BF16)
        else:
            done[i] = part[i].astype(BF16)
        stores.append(pltpu.make_async_copy(done.at[i], out_ref.at[i], out_sems.at[i]))
        stores[-1].start()
    for store in stores:
        store.wait()


def core_rows(core, g, *got):
    nz, nx, _, rows, cols = g.shape
    hbm = pl.BlockSpec(memory_space=pl.ANY)
    return pl.pallas_call(
        functools.partial(core_rows_kernel, bool(got)),
        in_specs=[pl.BlockSpec(memory_space=pltpu.SMEM), hbm] + [hbm for _ in got],
        out_specs=hbm,
        out_shape=jax.ShapeDtypeStruct((nx, nz, rows, cols), BF16),
        scratch_shapes=[
            pltpu.VMEM((nx, nz, rows, cols), F32),
            pltpu.VMEM((nx, nz, rows, cols), BF16),
            pltpu.VMEM((nx, nz, rows, cols), BF16),
            pltpu.SemaphoreType.DMA((nx,)),
            pltpu.SemaphoreType.DMA((nx,)),
            pltpu.SemaphoreType.DMA((nx,)),
        ],
        compiler_params=pltpu.CompilerParams(vmem_limit_bytes=VMEM_LIMIT),
    )(core[None].astype(jnp.int32), g, *got)


def decode_kernel(width, place, slots_ref, envs_ref, table_ref, gain_ref, *refs):
    n_pieces = 2 * len(PARTS) * NC
    heads, refs = refs[:NY], refs[NY:]
    pieces, (out_ref, w_ref, hidden, mixed, state, sems) = refs[:n_pieces], refs[n_pieces:]
    my_x, my_c, my_y = place[0], place[1], place[2]
    blocks, wide = w_ref.shape[0], w_ref.shape[-1]
    slots, own = slots_ref.shape[0], envs_ref.shape[0]
    m = slots + own
    tail = out_ref.shape[1] - slots
    copies = ([], [])
    for p in range(n_pieces):
        second, rest = divmod(p, len(PARTS) * NC)
        (k, begin, count), other = PARTS[rest // NC], rest % NC
        core = lax.rem(my_c + other, NC)
        for i in range(begin, begin + count):
            x_off, y_off = (k, i) if second else (i, k)
            x = lax.rem(my_x - x_off + NX, NX)
            y = lax.rem(my_y - y_off + NY, NY)
            copy = pltpu.make_async_copy(
                pieces[p].at[i - begin],
                w_ref.at[2 * y + second, :, x, core],
                sems.at[((second * NX + k) * NX + i) * NC + other],
            )
            copy.start()
            copies[second].append(copy)

    actions = table_ref.shape[0]
    number = lax.broadcasted_iota(jnp.int32, (m, actions), 1) + 1
    lanes = 128

    def onehot(step):
        tags = [ref[:, width:].astype(F32) for ref in (slots_ref, envs_ref)]
        tags = jnp.concatenate(tags, 0)
        chosen = lax.broadcasted_iota(jnp.int32, tags.shape, 1) == step
        tag = jnp.sum(jnp.where(chosen, tags, 0.0), axis=1, keepdims=True).astype(jnp.int32)
        return jnp.where(tag == number, 1.0, 0.0).astype(BF16)

    def embed(hot, cols, old):
        embedded = jnp.dot(hot, table_ref[:, cols], preferred_element_type=F32)
        hidden[:, cols] = (old.astype(F32) + embedded).astype(BF16)

    hot = onehot(0)
    for n in range(blocks):
        cols = slice(n * wide, (n + 1) * wide)
        state[:slots, cols] = slots_ref[:, cols]
        state[slots:, cols] = envs_ref[:, cols]
        embed(hot, cols, state[:, cols])
    for copy in copies[0] + copies[1]:
        copy.wait()

    def control_step(step, carry):
        total = jnp.zeros((m, lanes), F32)
        for n in range(blocks):
            w = w_ref[n].reshape(width, wide)
            got = jnp.dot(hidden[...], w, preferred_element_type=F32).astype(BF16)
            mixed[:, n * wide : (n + 1) * wide] = got
            got = got.astype(F32)
            for at in range(0, wide, lanes):
                total = total + got[:, at : at + lanes] * got[:, at : at + lanes]
        total = jnp.sum(total, axis=1, keepdims=True)
        inverse = lax.rsqrt(total * (1.0 / width) + norm_eps)
        hot = onehot(step + 1)
        for n in range(blocks):
            cols = slice(n * wide, (n + 1) * wide)
            old = state[:, cols].astype(F32)
            new = old + gain_ref[:, cols] * mixed[:, cols].astype(F32) * inverse
            new = new.astype(BF16)
            state[:, cols] = new
            embed(hot, cols, new)
        return carry

    lax.fori_loop(0, STEPS, control_step, 0)
    for y in range(NY):
        out_ref[y, :slots, :] = state[:slots, 2 * y * wide : 2 * (y + 1) * wide]
    for k in range(NY):
        scores = lax.dot_general(
            state[slots:m, :],
            heads[k][...],
            (((1,), (1,)), ((), ())),
            preferred_element_type=F32,
        )
        row = my_y * own + lax.broadcasted_iota(jnp.int32, scores.shape, 0)
        scores = (scores * jnp.where(row < place[3], 1.0, 0.0)).astype(BF16)
        packed = [scores[i * tail : (i + 1) * tail] for i in range(own // tail)]
        out_ref[lax.rem(my_y + k, NY), slots:, :] = jnp.concatenate(packed, 1)


def decode(place, slot_rows, env_rows, table, gain, heads, pieces):
    slots, own, width = slot_rows.shape[0], env_rows.shape[0], table.shape[1]
    wide, m = width // NY // 2, slots + own
    tail = own * heads[0].shape[0] // (width // NY)
    vmem = pl.BlockSpec(memory_space=pltpu.VMEM)
    return pl.pallas_call(
        functools.partial(decode_kernel, width),
        in_specs=[pl.BlockSpec(memory_space=pltpu.SMEM)]
        + [vmem] * (4 + NY)
        + [pl.BlockSpec(memory_space=pl.ANY)] * len(pieces),
        out_specs=vmem,
        out_shape=jax.ShapeDtypeStruct((NY, slots + tail, width // NY), BF16),
        scratch_shapes=[
            pltpu.VMEM((2 * NY, NZ, NX, NC, width // (NZ * NX * NC), wide), BF16),
            pltpu.VMEM((m, width), BF16),
            pltpu.VMEM((m, width), BF16),
            pltpu.VMEM((m, width), BF16),
            pltpu.SemaphoreType.DMA((2 * NX * NX * NC,)),
        ],
        compiler_params=pltpu.CompilerParams(vmem_limit_bytes=VMEM_LIMIT),
        cost_estimate=pl.CostEstimate(
            flops=2 * STEPS * m * width * width, bytes_accessed=2 * width * width, transcendentals=0
        ),
    )(place, slot_rows, env_rows, table, gain, *heads, *pieces)


def body(
    grad_parts,
    master,
    moment_one,
    moment_two,
    states,
    action_ids,
    env_counts,
    owners,
    act_table,
    norm_gain,
    head,
):
    width, cols = grad_parts.shape[1:]
    rows = width // (NZ * NX * NC)
    half = cols // 2
    env_slots = states.shape[0]
    owner_num = NZ * NX * NC
    capacity = max(2, 3 * env_slots // (2 * owner_num))
    share = capacity // NY
    slots = owner_num * share
    own = env_slots // NY
    my_x, my_c, my_y = lax.axis_index("x"), lax.axis_index("c"), lax.axis_index("y")
    place = jnp.stack([my_x, my_c, my_y, env_counts[0]]).astype(jnp.int32)

    g = grad_parts[0].reshape(NZ, NX, NC, rows, cols)
    both = core_rows(my_c, g, swap(core_rows(1 - my_c, g)))
    both, head = lax.optimization_barrier((both, head))
    by_x = exchange(both, "x")
    head = head.T
    heads = [head, shift(head, "y", 3, NY), None, shift(head, "y", 1, NY)]
    by_x, heads[1], heads[3], states, head = lax.optimization_barrier(
        (by_x, heads[1], heads[3], states, head)
    )
    heads[2] = shift(head, "y", 2, NY)
    by_x = by_x.astype(F32).sum(0).astype(BF16)
    gradient = exchange(by_x, "z").astype(F32).sum(0)

    active = jnp.arange(env_slots, dtype=jnp.int32) < env_counts[0]
    target = owners[:, 0]
    marks = (
        (target[:, None] == jnp.arange(owner_num, dtype=jnp.int32)[None, :]) & active[:, None]
    ).astype(jnp.int32)
    ranked = jnp.cumsum(marks, axis=0) - marks
    slot_idx = jnp.sum(ranked * marks, axis=1)
    mine = active & (slot_idx // share == my_y)
    column = target // NC % NX
    ahead = lax.rem(column - my_x + NX, NX)
    group = target // (NC * NX) * NC + target % NC
    groups = NZ * NC
    index = jnp.where(mine, (ahead * groups + group - my_y) * share + slot_idx, -1)
    pick = (jnp.arange(slots, dtype=jnp.int32)[:, None] == index[None, :]).astype(BF16)
    tags = jnp.pad((action_ids + 1).astype(BF16), ((0, 0), (0, TAGS - STEPS)))
    tagged = jnp.concatenate([states, tags], 1)
    outgoing = jnp.dot(pick, tagged, preferred_element_type=F32).astype(BF16)
    span = groups * share
    outgoing = [shift(outgoing[k * span : (k + 1) * span], "x", k, NX) for k in range(NX)]
    deep = -(-NX * share // 16) * 16
    row = jnp.arange(groups * deep, dtype=jnp.int32)
    place_in, part = row % deep, row // deep
    from_row = place_in // share * span + part * share + place_in % share
    from_row = jnp.where(place_in < NX * share, from_row, -1)
    pick = (from_row[:, None] == jnp.arange(slots, dtype=jnp.int32)[None, :]).astype(BF16)
    outgoing = jnp.dot(pick, jnp.concatenate(outgoing, 0), preferred_element_type=F32)
    outgoing = outgoing.astype(BF16).reshape(groups, deep, width + TAGS)
    actor_rows = lax.dynamic_slice_in_dim(tagged, my_y * own, own, 0)

    m_new = beta_one * moment_one + (1.0 - beta_one) * gradient
    v_new = beta_two * moment_two + (1.0 - beta_two) * gradient * gradient
    w_new = master - rate_lr * (m_new / corr_one) / (jnp.sqrt(v_new / corr_two) + adam_eps)

    w = exchange(jnp.broadcast_to(w_new.astype(BF16)[None], (NZ, rows, cols)), "z")
    w, outgoing, actor_rows, heads = lax.optimization_barrier((w, outgoing, actor_rows, heads))
    first, second = w[..., :half], w[..., half:]
    first = jnp.stack([shift(first, "x", k, NX) for k in range(NX)])
    second = jnp.stack([shift(second, "y", k, NY) for k in range(NY)])
    arrived = exchange(outgoing, ("z", "c")).reshape(groups * deep, width + TAGS)
    row = jnp.arange(slots, dtype=jnp.int32)
    source, behind = row // share, lax.rem(my_x - row // share // NC % NX + NX, NX)
    from_row = (source // (NC * NX) * NC + source % NC) * deep + behind * share + row % share
    pick = (from_row[:, None] == jnp.arange(groups * deep, dtype=jnp.int32)[None, :]).astype(BF16)
    slot_rows = jnp.dot(pick, arrived, preferred_element_type=F32).astype(BF16)
    first, second = lax.optimization_barrier((first, second))
    near = [shift(v, axis, k, NX) for v, axis in ((first, "y"), (second, "x")) for k in (1, 3)]
    near = lax.optimization_barrier(near)
    far = []
    for (back, front), axis in ((near[:2], "y"), (near[2:], "x")):
        far += [shift(back[: NX // 2], axis, 1, NX), shift(front[NX // 2 :], axis, 3, NX)]
    far, slot_rows = lax.optimization_barrier((far, slot_rows))
    pieces = []
    for piece in [first, *near[:2], *far[:2], second, *near[2:], *far[2:]]:
        pieces += [piece, swap(piece)]

    final = decode(place, slot_rows, actor_rows, act_table, norm_gain[None, :], heads, pieces)
    landed = exchange(final, "y")

    each = head.shape[0]
    scores = landed[:, slots:].astype(F32).reshape(NY, -1, cols // each, each)
    logits = jnp.transpose(scores, (0, 2, 1, 3)).reshape(env_slots, each)

    row = jnp.arange(owner_num * capacity, dtype=jnp.int32)
    at = row % capacity // share * slots + row // capacity * share + row % share
    order = (at[:, None] == row[None, :]).astype(BF16)
    landed = landed[:, :slots].reshape(owner_num * capacity, cols)
    received = jnp.dot(order, landed, preferred_element_type=F32)
    return (m_new, v_new, w_new, logits, received.astype(BF16))


def solution(mesh):
    grid = Mesh(mesh.devices.reshape(NZ, NX, NC, NY), DP + ("y",))
    in_specs = (
        P(DP, None, "y"),
        P(DP, "y"),
        P(DP, "y"),
        P(DP, "y"),
        P(DP, None),
        P(DP, None),
        P(DP),
        P(DP, None),
        P(),
        P(),
        P(None, "y"),
    )
    out_specs = (P(DP, "y"),) * 5
    return jax.shard_map(body, mesh=grid, in_specs=in_specs, out_specs=out_specs, check_vma=False)
```

```python
import functools

import jax
import jax.numpy as jnp
from jax import lax
from jax.experimental import pallas as pl
from jax.experimental.pallas import tpu as pltpu
from jax.sharding import Mesh, PartitionSpec as P

STEPS = 4
NZ, NX, NC, NY = 8, 4, 2, 4
DP = ("z", "x", "c")
TAGS = 128
VMEM_LIMIT = 60 * 2**20
PARTS = ((0, 0, 4), (1, 0, 4), (3, 0, 4), (2, 0, 2), (2, 2, 2))

beta_one = 0.9
beta_two = 0.999
corr_one = 1.0 - 0.9**10
corr_two = 1.0 - 0.999**10
rate_lr = 0.01
adam_eps = 1e-08
norm_eps = 1e-06
F32 = jnp.float32
BF16 = jnp.bfloat16


def exchange(v, axis):
    return lax.all_to_all(v, axis, 0, 0, tiled=True)


def shift(v, axis, k, n):
    if k == 0:
        return v
    return lax.ppermute(v, axis, [(i, (i + k) % n) for i in range(n)])


def swap(v):
    return shift(v, "c", 1, NC)


def core_rows_kernel(add, core, g_ref, *refs):
    if add:
        got_ref, refs = refs[0], refs[1:]
    out_ref, part, got, done, in_sems, got_sems, out_sems = refs
    nx = part.shape[0]
    loads, extra, stores = [], [], []
    for i in range(nx):
        loads.append(pltpu.make_async_copy(g_ref.at[:, i, core[0]], part.at[i], in_sems.at[i]))
        loads[-1].start()
        if add:
            extra.append(pltpu.make_async_copy(got_ref.at[i], got.at[i], got_sems.at[i]))
            extra[-1].start()
    for i in range(nx):
        loads[i].wait()
        if add:
            extra[i].wait()
            done[i] = (part[i] + got[i].astype(F32)).astype(BF16)
        else:
            done[i] = part[i].astype(BF16)
        stores.append(pltpu.make_async_copy(done.at[i], out_ref.at[i], out_sems.at[i]))
        stores[-1].start()
    for store in stores:
        store.wait()


def core_rows(core, g, *got):
    nz, nx, _, rows, cols = g.shape
    hbm = pl.BlockSpec(memory_space=pl.ANY)
    return pl.pallas_call(
        functools.partial(core_rows_kernel, bool(got)),
        in_specs=[pl.BlockSpec(memory_space=pltpu.SMEM), hbm] + [hbm for _ in got],
        out_specs=hbm,
        out_shape=jax.ShapeDtypeStruct((nx, nz, rows, cols), BF16),
        scratch_shapes=[
            pltpu.VMEM((nx, nz, rows, cols), F32),
            pltpu.VMEM((nx, nz, rows, cols), BF16),
            pltpu.VMEM((nx, nz, rows, cols), BF16),
            pltpu.SemaphoreType.DMA((nx,)),
            pltpu.SemaphoreType.DMA((nx,)),
            pltpu.SemaphoreType.DMA((nx,)),
        ],
        compiler_params=pltpu.CompilerParams(vmem_limit_bytes=57 * 2**20),
    )(core[None].astype(jnp.int32), g, *got)


def decode_kernel(width, place, slots_ref, envs_ref, table_from, gain_ref, *refs):
    n_pieces = 2 * len(PARTS) * NC
    heads_from, refs = refs[:NY], refs[NY:]
    pieces, refs = refs[:n_pieces], refs[n_pieces:]
    out_ref, w_ref, hidden, mixed, state, tags_ref, table_ref, heads, sems, row_sems = refs
    my_x, my_c, my_y = place[0], place[1], place[2]
    blocks, wide = w_ref.shape[0], w_ref.shape[-1]
    slots, own = slots_ref.shape[0], envs_ref.shape[0]
    m = slots + own
    tail = out_ref.shape[1] - slots
    early = [
        (slots_ref.at[:, :width], state.at[:slots]),
        (envs_ref.at[:, :width], state.at[slots:]),
        (slots_ref.at[:, width:], tags_ref.at[:slots]),
        (envs_ref.at[:, width:], tags_ref.at[slots:]),
        (table_from, table_ref),
    ]
    late = [(heads_from[k], heads.at[k]) for k in range(NY)]
    early, late = (
        [pltpu.make_async_copy(a, b, row_sems.at[base + i]) for i, (a, b) in enumerate(group)]
        for group, base in ((early, 0), (late, len(early)))
    )
    for copy in early:
        copy.start()
    copies = []
    for p in range(n_pieces):
        second, rest = divmod(p, len(PARTS) * NC)
        (k, begin, count), other = PARTS[rest // NC], rest % NC
        core = lax.rem(my_c + other, NC)
        for i in range(begin, begin + count):
            x_off, y_off = (k, i) if second else (i, k)
            x = lax.rem(my_x - x_off + NX, NX)
            y = lax.rem(my_y - y_off + NY, NY)
            copy = pltpu.make_async_copy(
                pieces[p].at[i - begin],
                w_ref.at[2 * y + second, :, x, core],
                sems.at[((second * NX + k) * NX + i) * NC + other],
            )
            copy.start()
            copies.append(copy)

    actions = table_ref.shape[0]
    number = lax.broadcasted_iota(jnp.int32, (m, actions), 1) + 1
    lanes = 128

    def onehot(step):
        tags = tags_ref[...].astype(F32)
        chosen = lax.broadcasted_iota(jnp.int32, tags.shape, 1) == step
        tag = jnp.sum(jnp.where(chosen, tags, 0.0), axis=1, keepdims=True).astype(jnp.int32)
        return jnp.where(tag == number, 1.0, 0.0).astype(BF16)

    def embed(hot, cols, old):
        embedded = jnp.dot(hot, table_ref[:, cols], preferred_element_type=F32)
        hidden[:, cols] = (old.astype(F32) + embedded).astype(BF16)

    for copy in late:
        copy.start()
    for copy in early:
        copy.wait()
    hot = onehot(0)
    for n in range(blocks):
        cols = slice(n * wide, (n + 1) * wide)
        embed(hot, cols, state[:, cols])
    for copy in copies + late:
        copy.wait()

    def control_step(step, carry):
        total = jnp.zeros((m, lanes), F32)
        for n in range(blocks):
            w = w_ref[n].reshape(width, wide)
            got = jnp.dot(hidden[...], w, preferred_element_type=F32).astype(BF16)
            mixed[:, n * wide : (n + 1) * wide] = got
            got = got.astype(F32)
            for at in range(0, wide, lanes):
                total = total + got[:, at : at + lanes] * got[:, at : at + lanes]
        total = jnp.sum(total, axis=1, keepdims=True)
        inverse = lax.rsqrt(total * (1.0 / width) + norm_eps)
        hot = onehot(step + 1)
        for n in range(blocks):
            cols = slice(n * wide, (n + 1) * wide)
            old = state[:, cols].astype(F32)
            new = old + gain_ref[:, cols] * mixed[:, cols].astype(F32) * inverse
            new = new.astype(BF16)
            state[:, cols] = new
            embed(hot, cols, new)
        return carry

    lax.fori_loop(0, STEPS, control_step, 0)
    for y in range(NY):
        out_ref[y, :slots, :] = state[:slots, 2 * y * wide : 2 * (y + 1) * wide]
    for k in range(NY):
        scores = lax.dot_general(
            heads[k],
            state[slots:m, :],
            (((1,), (1,)), ((), ())),
            preferred_element_type=F32,
        )
        row = my_y * own + lax.broadcasted_iota(jnp.int32, scores.shape, 1)
        scores = (scores * jnp.where(row < place[3], 1.0, 0.0)).astype(BF16)
        packed = [scores[i * tail : (i + 1) * tail] for i in range(scores.shape[0] // tail)]
        out_ref[lax.rem(my_y + k, NY), slots:, :] = jnp.concatenate(packed, 1)


def decode(place, slot_rows, env_rows, table, gain, heads, pieces):
    slots, own, width = slot_rows.shape[0], env_rows.shape[0], table.shape[1]
    wide, m = width // NY // 2, slots + own
    tail = own * heads[0].shape[0] // (width // NY)
    vmem, hbm = pl.BlockSpec(memory_space=pltpu.VMEM), pl.BlockSpec(memory_space=pl.ANY)
    return pl.pallas_call(
        functools.partial(decode_kernel, width),
        in_specs=[pl.BlockSpec(memory_space=pltpu.SMEM)]
        + [hbm] * 3
        + [vmem]
        + [hbm] * (NY + len(pieces)),
        out_specs=vmem,
        out_shape=jax.ShapeDtypeStruct((NY, slots + tail, width // NY), BF16),
        scratch_shapes=[
            pltpu.VMEM((2 * NY, NZ, NX, NC, width // (NZ * NX * NC), wide), BF16),
            pltpu.VMEM((m, width), BF16),
            pltpu.VMEM((m, width), BF16),
            pltpu.VMEM((m, width), BF16),
            pltpu.VMEM((m, TAGS), BF16),
            pltpu.VMEM(table.shape, BF16),
            pltpu.VMEM((NY, *heads[0].shape), BF16),
            pltpu.SemaphoreType.DMA((2 * NX * NX * NC,)),
            pltpu.SemaphoreType.DMA((5 + NY,)),
        ],
        compiler_params=pltpu.CompilerParams(vmem_limit_bytes=VMEM_LIMIT),
        cost_estimate=pl.CostEstimate(
            flops=2 * STEPS * m * width * width, bytes_accessed=2 * width * width, transcendentals=0
        ),
    )(place, slot_rows, env_rows, table, gain, *heads, *pieces)


def body(
    grad_parts,
    master,
    moment_one,
    moment_two,
    states,
    action_ids,
    env_counts,
    owners,
    act_table,
    norm_gain,
    head,
):
    width, cols = grad_parts.shape[1:]
    rows = width // (NZ * NX * NC)
    half = cols // 2
    env_slots = states.shape[0]
    owner_num = NZ * NX * NC
    capacity = max(2, 3 * env_slots // (2 * owner_num))
    share = capacity // NY
    slots = owner_num * share
    own = env_slots // NY
    my_x, my_c, my_y = lax.axis_index("x"), lax.axis_index("c"), lax.axis_index("y")
    place = jnp.stack([my_x, my_c, my_y, env_counts[0]]).astype(jnp.int32)

    g = grad_parts[0].reshape(NZ, NX, NC, rows, cols)
    both = core_rows(my_c, g, swap(core_rows(1 - my_c, g)))
    both, head, place = lax.optimization_barrier((both, head, place))
    by_x = exchange(both, "x")
    head = head.T
    heads = [head, shift(head, "y", 3, NY), None, shift(head, "y", 1, NY)]
    by_x, heads[1], heads[3], states, head = lax.optimization_barrier(
        (by_x, heads[1], heads[3], states, head)
    )
    heads[2] = shift(head, "y", 2, NY)
    by_x = by_x.astype(F32).sum(0).astype(BF16)
    gradient = exchange(by_x, "z").astype(F32).sum(0)

    active = jnp.arange(env_slots, dtype=jnp.int32) < env_counts[0]
    target = owners[:, 0]
    marks = (
        (target[:, None] == jnp.arange(owner_num, dtype=jnp.int32)[None, :]) & active[:, None]
    ).astype(jnp.int32)
    ranked = jnp.cumsum(marks, axis=0) - marks
    slot_idx = jnp.sum(ranked * marks, axis=1)
    mine = active & (slot_idx // share == my_y)
    column = target // NC % NX
    ahead = lax.rem(column - my_x + NX, NX)
    group = target // (NC * NX) * NC + target % NC
    groups = NZ * NC
    index = jnp.where(mine, (ahead * groups + group - my_y) * share + slot_idx, -1)
    pick = (jnp.arange(slots, dtype=jnp.int32)[:, None] == index[None, :]).astype(BF16)
    tags = jnp.pad((action_ids + 1).astype(BF16), ((0, 0), (0, TAGS - STEPS)))
    tagged = jnp.concatenate([states, tags], 1)
    outgoing = jnp.dot(pick, tagged, preferred_element_type=F32).astype(BF16)
    span = groups * share
    outgoing = [shift(outgoing[k * span : (k + 1) * span], "x", k, NX) for k in range(NX)]
    deep = -(-NX * share // 16) * 16
    row = jnp.arange(groups * deep, dtype=jnp.int32)
    place_in, part = row % deep, row // deep
    from_row = place_in // share * span + part * share + place_in % share
    from_row = jnp.where(place_in < NX * share, from_row, -1)
    pick = (from_row[:, None] == jnp.arange(slots, dtype=jnp.int32)[None, :]).astype(BF16)
    outgoing = jnp.dot(pick, jnp.concatenate(outgoing, 0), preferred_element_type=F32)
    outgoing = outgoing.astype(BF16).reshape(groups, deep, width + TAGS)
    actor_rows = lax.dynamic_slice_in_dim(tagged, my_y * own, own, 0)

    m_new = beta_one * moment_one + (1.0 - beta_one) * gradient
    v_new = beta_two * moment_two + (1.0 - beta_two) * gradient * gradient
    w_new = master - rate_lr * (m_new / corr_one) / (jnp.sqrt(v_new / corr_two) + adam_eps)

    w = exchange(jnp.broadcast_to(w_new.astype(BF16)[None], (NZ, rows, cols)), "z")
    w, outgoing, actor_rows, heads = lax.optimization_barrier((w, outgoing, actor_rows, heads))
    first, second = w[..., :half], w[..., half:]
    first = jnp.stack([shift(first, "x", k, NX) for k in range(NX)])
    second = jnp.stack([shift(second, "y", k, NY) for k in range(NY)])
    arrived = exchange(outgoing, ("z", "c")).reshape(groups * deep, width + TAGS)
    row = jnp.arange(slots, dtype=jnp.int32)
    source, behind = row // share, lax.rem(my_x - row // share // NC % NX + NX, NX)
    from_row = (source // (NC * NX) * NC + source % NC) * deep + behind * share + row % share
    pick = (from_row[:, None] == jnp.arange(groups * deep, dtype=jnp.int32)[None, :]).astype(BF16)
    slot_rows = jnp.dot(pick, arrived, preferred_element_type=F32).astype(BF16)
    first, second = lax.optimization_barrier((first, second))
    near = [shift(v, axis, k, NX) for v, axis in ((first, "y"), (second, "x")) for k in (1, 3)]
    near = lax.optimization_barrier(near)
    far = []
    for (back, front), axis in ((near[:2], "y"), (near[2:], "x")):
        far += [shift(back[: NX // 2], axis, 1, NX), shift(front[NX // 2 :], axis, 3, NX)]
    far, slot_rows = lax.optimization_barrier((far, slot_rows))
    pieces = []
    for piece in [first, *near[:2], *far[:2], second, *near[2:], *far[2:]]:
        pieces += [piece, swap(piece)]

    final = decode(place, slot_rows, actor_rows, act_table, norm_gain[None, :], heads, pieces)
    landed = exchange(final, "y")

    each = head.shape[0]
    scores = landed[:, slots:].astype(F32).reshape(NY, -1, cols // own, own)
    logits = jnp.transpose(scores, (2, 1, 0, 3)).reshape(each, env_slots).T

    row = jnp.arange(owner_num * capacity, dtype=jnp.int32)
    deep = landed.shape[1]
    at = row % capacity // share * deep + row // capacity * share + row % share
    order = (at[:, None] == jnp.arange(NY * deep, dtype=jnp.int32)[None, :]).astype(BF16)
    received = jnp.dot(order, landed.reshape(NY * deep, cols), preferred_element_type=F32)
    return (m_new, v_new, w_new, logits, received.astype(BF16))


def solution(mesh):
    grid = Mesh(mesh.devices.reshape(NZ, NX, NC, NY), DP + ("y",))
    in_specs = (
        P(DP, None, "y"),
        P(DP, "y"),
        P(DP, "y"),
        P(DP, "y"),
        P(DP, None),
        P(DP, None),
        P(DP),
        P(DP, None),
        P(),
        P(),
        P(None, "y"),
    )
    out_specs = (P(DP, "y"),) * 5
    return jax.shard_map(body, mesh=grid, in_specs=in_specs, out_specs=out_specs, check_vma=False)
```

```python
import functools

import jax
import jax.numpy as jnp
from jax import lax
from jax.experimental import pallas as pl
from jax.experimental.pallas import tpu as pltpu
from jax.sharding import Mesh, PartitionSpec as P

STEPS = 4
NZ, NX, NC, NY = 8, 4, 2, 4
DP = ("z", "x", "c")
TAGS = 128
VMEM_LIMIT = 60 * 2**20
PARTS = ((0, 0, 4), (1, 0, 4), (3, 0, 4), (2, 0, 2), (2, 2, 2))

beta_one = 0.9
beta_two = 0.999
corr_one = 1.0 - 0.9**10
corr_two = 1.0 - 0.999**10
rate_lr = 0.01
adam_eps = 1e-08
norm_eps = 1e-06
F32 = jnp.float32
BF16 = jnp.bfloat16


def exchange(v, axis):
    return lax.all_to_all(v, axis, 0, 0, tiled=True)


def shift(v, axis, k, n):
    if k == 0:
        return v
    return lax.ppermute(v, axis, [(i, (i + k) % n) for i in range(n)])


def swap(v):
    return shift(v, "c", 1, NC)


def core_rows_kernel(add, core, g_ref, *refs):
    if add:
        got_ref, refs = refs[0], refs[1:]
    out_ref, part, got, done, in_sems, got_sems, out_sems = refs
    nx = part.shape[0]
    loads, extra, stores = [], [], []
    for i in range(nx):
        loads.append(pltpu.make_async_copy(g_ref.at[:, i, core[0]], part.at[i], in_sems.at[i]))
        loads[-1].start()
        if add:
            extra.append(pltpu.make_async_copy(got_ref.at[i], got.at[i], got_sems.at[i]))
            extra[-1].start()
    for i in range(nx):
        loads[i].wait()
        if add:
            extra[i].wait()
            done[i] = (part[i] + got[i].astype(F32)).astype(BF16)
        else:
            done[i] = part[i].astype(BF16)
        stores.append(pltpu.make_async_copy(done.at[i], out_ref.at[i], out_sems.at[i]))
        stores[-1].start()
    for store in stores:
        store.wait()


def core_rows(core, g, *got):
    nz, nx, _, rows, cols = g.shape
    hbm = pl.BlockSpec(memory_space=pl.ANY)
    return pl.pallas_call(
        functools.partial(core_rows_kernel, bool(got)),
        in_specs=[pl.BlockSpec(memory_space=pltpu.SMEM), hbm] + [hbm for _ in got],
        out_specs=hbm,
        out_shape=jax.ShapeDtypeStruct((nx, nz, rows, cols), BF16),
        scratch_shapes=[
            pltpu.VMEM((nx, nz, rows, cols), F32),
            pltpu.VMEM((nx, nz, rows, cols), BF16),
            pltpu.VMEM((nx, nz, rows, cols), BF16),
            pltpu.SemaphoreType.DMA((nx,)),
            pltpu.SemaphoreType.DMA((nx,)),
            pltpu.SemaphoreType.DMA((nx,)),
        ],
        compiler_params=pltpu.CompilerParams(vmem_limit_bytes=57 * 2**20),
    )(core[None].astype(jnp.int32), g, *got)


def decode_kernel(width, place, slots_ref, envs_ref, table_from, gain_ref, *refs):
    n_pieces = 2 * len(PARTS) * NC
    heads_from, refs = refs[:NY], refs[NY:]
    pieces, refs = refs[:n_pieces], refs[n_pieces:]
    out_ref, w_ref, hidden, mixed, state, tags_ref, table_ref, heads, sems, row_sems = refs
    my_x, my_c, my_y = place[0], place[1], place[2]
    blocks, wide = w_ref.shape[0], w_ref.shape[-1]
    slots, own = slots_ref.shape[0], envs_ref.shape[0]
    m = slots + own
    tail = out_ref.shape[1] - slots
    early = [
        (slots_ref.at[:, :width], state.at[:slots]),
        (envs_ref.at[:, :width], state.at[slots:]),
        (slots_ref.at[:, width:], tags_ref.at[:slots]),
        (envs_ref.at[:, width:], tags_ref.at[slots:]),
        (table_from, table_ref),
    ]
    late = [(heads_from[k], heads.at[k]) for k in range(NY)]
    early, late = (
        [pltpu.make_async_copy(a, b, row_sems.at[base + i]) for i, (a, b) in enumerate(group)]
        for group, base in ((early, 0), (late, len(early)))
    )
    for copy in early:
        copy.start()
    copies = []
    for p in range(n_pieces):
        second, rest = divmod(p, len(PARTS) * NC)
        (k, begin, count), other = PARTS[rest // NC], rest % NC
        core = lax.rem(my_c + other, NC)
        for i in range(begin, begin + count):
            x_off, y_off = (k, i) if second else (i, k)
            x = lax.rem(my_x - x_off + NX, NX)
            y = lax.rem(my_y - y_off + NY, NY)
            copy = pltpu.make_async_copy(
                pieces[p].at[i - begin],
                w_ref.at[2 * y + second, :, x, core],
                sems.at[((second * NX + k) * NX + i) * NC + other],
            )
            copy.start()
            copies.append(copy)

    actions = table_ref.shape[0]
    number = lax.broadcasted_iota(jnp.int32, (m, actions), 1) + 1
    lanes = 128

    def onehot(step):
        tags = tags_ref[...].astype(F32)
        chosen = lax.broadcasted_iota(jnp.int32, tags.shape, 1) == step
        tag = jnp.sum(jnp.where(chosen, tags, 0.0), axis=1, keepdims=True).astype(jnp.int32)
        return jnp.where(tag == number, 1.0, 0.0).astype(BF16)

    def embed(hot, cols, old):
        embedded = jnp.dot(hot, table_ref[:, cols], preferred_element_type=F32)
        hidden[:, cols] = (old.astype(F32) + embedded).astype(BF16)

    for copy in late:
        copy.start()
    for copy in early:
        copy.wait()
    hot = onehot(0)
    for n in range(blocks):
        cols = slice(n * wide, (n + 1) * wide)
        embed(hot, cols, state[:, cols])
    for copy in copies + late:
        copy.wait()

    def control_step(step, last):
        total = jnp.zeros((m, lanes), F32)
        for n in range(blocks):
            w = w_ref[n].reshape(width, wide)
            got = jnp.dot(hidden[...], w, preferred_element_type=F32).astype(BF16)
            mixed[:, n * wide : (n + 1) * wide] = got
            got = got.astype(F32)
            for at in range(0, wide, lanes):
                total = total + got[:, at : at + lanes] * got[:, at : at + lanes]
        total = jnp.sum(total, axis=1, keepdims=True)
        inverse = lax.rsqrt(total * (1.0 / width) + norm_eps)
        hot = None if last else onehot(step + 1)
        for n in range(blocks):
            cols = slice(n * wide, (n + 1) * wide)
            old = state[:, cols].astype(F32)
            new = old + gain_ref[:, cols] * mixed[:, cols].astype(F32) * inverse
            new = new.astype(BF16)
            if last:
                out_cols = slice(n % 2 * wide, (n % 2 + 1) * wide)
                out_ref[n // 2, :slots, out_cols] = new[:slots]
                state[slots:, cols] = new[slots:]
            else:
                state[:, cols] = new
                embed(hot, cols, new)
        return 0

    lax.fori_loop(0, STEPS - 1, lambda step, _: control_step(step, False), 0)
    control_step(STEPS - 1, True)
    for k in range(NY):
        scores = lax.dot_general(
            heads[k],
            state[slots:m, :],
            (((1,), (1,)), ((), ())),
            preferred_element_type=F32,
        )
        row = my_y * own + lax.broadcasted_iota(jnp.int32, scores.shape, 1)
        scores = (scores * jnp.where(row < place[3], 1.0, 0.0)).astype(BF16)
        packed = [scores[i * tail : (i + 1) * tail] for i in range(scores.shape[0] // tail)]
        out_ref[lax.rem(my_y + k, NY), slots:, :] = jnp.concatenate(packed, 1)


def decode(place, slot_rows, env_rows, table, gain, heads, pieces):
    slots, own, width = slot_rows.shape[0], env_rows.shape[0], table.shape[1]
    wide, m = width // NY // 2, slots + own
    tail = own * heads[0].shape[0] // (width // NY)
    vmem, hbm = pl.BlockSpec(memory_space=pltpu.VMEM), pl.BlockSpec(memory_space=pl.ANY)
    return pl.pallas_call(
        functools.partial(decode_kernel, width),
        in_specs=[pl.BlockSpec(memory_space=pltpu.SMEM)]
        + [hbm] * 3
        + [vmem]
        + [hbm] * (NY + len(pieces)),
        out_specs=vmem,
        out_shape=jax.ShapeDtypeStruct((NY, slots + tail, width // NY), BF16),
        scratch_shapes=[
            pltpu.VMEM((2 * NY, NZ, NX, NC, width // (NZ * NX * NC), wide), BF16),
            pltpu.VMEM((m, width), BF16),
            pltpu.VMEM((m, width), BF16),
            pltpu.VMEM((m, width), BF16),
            pltpu.VMEM((m, TAGS), BF16),
            pltpu.VMEM(table.shape, BF16),
            pltpu.VMEM((NY, *heads[0].shape), BF16),
            pltpu.SemaphoreType.DMA((2 * NX * NX * NC,)),
            pltpu.SemaphoreType.DMA((5 + NY,)),
        ],
        compiler_params=pltpu.CompilerParams(vmem_limit_bytes=VMEM_LIMIT),
        cost_estimate=pl.CostEstimate(
            flops=2 * STEPS * m * width * width, bytes_accessed=2 * width * width, transcendentals=0
        ),
    )(place, slot_rows, env_rows, table, gain, *heads, *pieces)


def body(
    grad_parts,
    master,
    moment_one,
    moment_two,
    states,
    action_ids,
    env_counts,
    owners,
    act_table,
    norm_gain,
    head,
):
    width, cols = grad_parts.shape[1:]
    rows = width // (NZ * NX * NC)
    half = cols // 2
    env_slots = states.shape[0]
    owner_num = NZ * NX * NC
    capacity = max(2, 3 * env_slots // (2 * owner_num))
    share = capacity // NY
    slots = owner_num * share
    own = env_slots // NY
    my_x, my_c, my_y = lax.axis_index("x"), lax.axis_index("c"), lax.axis_index("y")
    place = jnp.stack([my_x, my_c, my_y, env_counts[0]]).astype(jnp.int32)

    g = grad_parts[0].reshape(NZ, NX, NC, rows, cols)
    both = core_rows(my_c, g, swap(core_rows(1 - my_c, g)))
    both, head, place = lax.optimization_barrier((both, head, place))
    by_x = exchange(both, "x")
    head = head.T
    heads = [head, shift(head, "y", 3, NY), None, shift(head, "y", 1, NY)]
    by_x, heads[1], heads[3], states, head = lax.optimization_barrier(
        (by_x, heads[1], heads[3], states, head)
    )
    heads[2] = shift(head, "y", 2, NY)
    by_x = by_x.astype(F32).sum(0).astype(BF16)
    gradient = exchange(by_x, "z").astype(F32).sum(0)

    active = jnp.arange(env_slots, dtype=jnp.int32) < env_counts[0]
    target = owners[:, 0]
    marks = (
        (target[:, None] == jnp.arange(owner_num, dtype=jnp.int32)[None, :]) & active[:, None]
    ).astype(jnp.int32)
    ranked = jnp.cumsum(marks, axis=0) - marks
    slot_idx = jnp.sum(ranked * marks, axis=1)
    mine = active & (slot_idx // share == my_y)
    column = target // NC % NX
    ahead = lax.rem(column - my_x + NX, NX)
    group = target // (NC * NX) * NC + target % NC
    groups = NZ * NC
    index = jnp.where(mine, (ahead * groups + group - my_y) * share + slot_idx, -1)
    pick = (jnp.arange(slots, dtype=jnp.int32)[:, None] == index[None, :]).astype(BF16)
    tags = jnp.pad((action_ids + 1).astype(BF16), ((0, 0), (0, TAGS - STEPS)))
    tagged = jnp.concatenate([states, tags], 1)
    outgoing = jnp.dot(pick, tagged, preferred_element_type=F32).astype(BF16)
    span = groups * share
    outgoing = [shift(outgoing[k * span : (k + 1) * span], "x", k, NX) for k in range(NX)]
    deep = -(-NX * share // 16) * 16
    row = jnp.arange(groups * deep, dtype=jnp.int32)
    place_in, part = row % deep, row // deep
    from_row = place_in // share * span + part * share + place_in % share
    from_row = jnp.where(place_in < NX * share, from_row, -1)
    pick = (from_row[:, None] == jnp.arange(slots, dtype=jnp.int32)[None, :]).astype(BF16)
    outgoing = jnp.dot(pick, jnp.concatenate(outgoing, 0), preferred_element_type=F32)
    outgoing = outgoing.astype(BF16).reshape(groups, deep, width + TAGS)
    actor_rows = lax.dynamic_slice_in_dim(tagged, my_y * own, own, 0)

    m_new = beta_one * moment_one + (1.0 - beta_one) * gradient
    v_new = beta_two * moment_two + (1.0 - beta_two) * gradient * gradient
    w_new = master - rate_lr * (m_new / corr_one) / (jnp.sqrt(v_new / corr_two) + adam_eps)

    w = exchange(jnp.broadcast_to(w_new.astype(BF16)[None], (NZ, rows, cols)), "z")
    w, outgoing, actor_rows, heads = lax.optimization_barrier((w, outgoing, actor_rows, heads))
    first, second = w[..., :half], w[..., half:]
    first = jnp.stack([shift(first, "x", k, NX) for k in range(NX)])
    second = jnp.stack([shift(second, "y", k, NY) for k in range(NY)])
    arrived = exchange(outgoing, ("z", "c")).reshape(groups * deep, width + TAGS)
    row = jnp.arange(slots, dtype=jnp.int32)
    source, behind = row // share, lax.rem(my_x - row // share // NC % NX + NX, NX)
    from_row = (source // (NC * NX) * NC + source % NC) * deep + behind * share + row % share
    pick = (from_row[:, None] == jnp.arange(groups * deep, dtype=jnp.int32)[None, :]).astype(BF16)
    slot_rows = jnp.dot(pick, arrived, preferred_element_type=F32).astype(BF16)
    first, second = lax.optimization_barrier((first, second))
    near = [shift(v, axis, k, NX) for v, axis in ((first, "y"), (second, "x")) for k in (1, 3)]
    near = lax.optimization_barrier(near)
    far = []
    for (back, front), axis in ((near[:2], "y"), (near[2:], "x")):
        far += [shift(back[: NX // 2], axis, 1, NX), shift(front[NX // 2 :], axis, 3, NX)]
    far, slot_rows = lax.optimization_barrier((far, slot_rows))
    pieces = []
    for piece in [first, *near[:2], *far[:2], second, *near[2:], *far[2:]]:
        pieces += [piece, swap(piece)]

    final = decode(place, slot_rows, actor_rows, act_table, norm_gain[None, :], heads, pieces)
    landed = exchange(final, "y")

    each = head.shape[0]
    scores = landed[:, slots:].astype(F32).reshape(NY, -1, cols // own, own)
    logits = jnp.transpose(scores, (2, 1, 0, 3)).reshape(each, env_slots).T

    row = jnp.arange(owner_num * capacity, dtype=jnp.int32)
    deep = landed.shape[1]
    at = row % capacity // share * deep + row // capacity * share + row % share
    order = (at[:, None] == jnp.arange(NY * deep, dtype=jnp.int32)[None, :]).astype(BF16)
    received = jnp.dot(order, landed.reshape(NY * deep, cols), preferred_element_type=F32)
    return (m_new, v_new, w_new, logits, received.astype(BF16))


def solution(mesh):
    grid = Mesh(mesh.devices.reshape(NZ, NX, NC, NY), DP + ("y",))
    in_specs = (
        P(DP, None, "y"),
        P(DP, "y"),
        P(DP, "y"),
        P(DP, "y"),
        P(DP, None),
        P(DP, None),
        P(DP),
        P(DP, None),
        P(),
        P(),
        P(None, "y"),
    )
    out_specs = (P(DP, "y"),) * 5
    return jax.shard_map(body, mesh=grid, in_specs=in_specs, out_specs=out_specs, check_vma=False)
```
